128 devices in a mesh: qa: 8 (over x, z_hi), qb: 16 (over y, z_lo, core).
Axes of the slice: x: 4, y: 4, z: 4 (z_hi: 2, z_lo: 2; z = z_hi * 2 + z_lo), core: 2. Of those that a mesh axis runs over, the one named last changes fastest.
Arguments:
- amplitudes: float32 [8, 16, 262144], P('qa', 'qb'), may hold values from -6 to 6
- gate_angles: float32 [2, 4, 7], replicated, may hold values from -3.140625 to 3.140625
- pair_masks: int32 [2, 4], replicated, may hold values from 0 to 2097151
- control_qubits: int32 [2, 4], replicated, may hold values from 0 to 24
- final_angles: float32 [4], replicated, may hold values from -3.140625 to 3.140625
Outputs:
- final_state: float32 [8, 16, 262144], P('qa', 'qb')
The draws below stay inside these ranges and needn't reach their ends.
Inputs may be any that keep to these rules, and one draw needn't show every extreme that they name: `pair_masks`: bit p of a mask selects the p-th pair of the gate's seven qubits; every bit is set in some draws. `control_qubits`: any qubit, inside or outside the gate's own seven; a control on the first qubit itself is a Z on it.
All inputs are finite; a program needn't handle non-finite values.
Results may differ from the reference program's by a relative error of at most 0.00014.
Values sent between devices are 32-bit elements; how exact they have to be, the bound alone decides.
A program may use at most 64 MiB of HBM per device.

```python
import jax
import jax.numpy as jnp
import numpy as np
from jax import lax

LOCAL_QUBITS = 18
LAYERS = 2
LOCAL = 262144
QB_BITS = 4
NQUBITS = 25
N_QA = 8
N_QB = 16


def set_ends(entries, key, least, largest):
    index_at = [jax.random.randint(jax.random.fold_in(key, axis), (), 0, length) for axis, length in enumerate(entries.shape)]
    main_axis = entries.shape.index(max(entries.shape))
    neighbour = index_at[:main_axis] + [(index_at[main_axis] + 1) % entries.shape[main_axis]] + index_at[main_axis + 1:]
    return entries.at[tuple(index_at)].set(least).at[tuple(neighbour)].set(largest)


def level_of(key, dims, pieces, low, top_value):
    level, own = 1.0, jax.random.fold_in(key, 6)
    for dim, parts in pieces:
        heights = jnp.exp(jax.random.uniform(jax.random.fold_in(own, dim), (parts,), jnp.float32, low / len(pieces), top_value / len(pieces)))
        level = level * jnp.repeat(heights, dims[dim] // parts).reshape([-1 if axis == dim else 1 for axis in range(len(dims))])
    return level


def normal_values(key, dims, deviation, most, cuts=(), held_as=jnp.bfloat16):
    values = jax.random.normal(key, dims, jnp.float32) * deviation
    if len(cuts) > 0:
        values = level_of(key, dims, cuts, -0.22, 0.18) * values
    return jnp.clip(values, min=-most, max=most).astype(held_as)


def setup_inputs(seed: int = 0) -> dict:
    key_list = jax.random.split(jax.random.key(seed), 6)
    amplitudes = normal_values(key_list[0], (N_QA, N_QB, LOCAL), 1.0, 6.0, ((0, 8), (1, 16)), jnp.float32)
    gate_angles = jnp.clip(jax.random.uniform(key_list[1], (LAYERS, 4, 7), jnp.float32, -3.140625, 3.140625), -3.140625, 3.140625)
    pair_masks = set_ends(jax.random.randint(key_list[2], (LAYERS, 4), 0, 2097152), jax.random.fold_in(key_list[2], 1), 0, 2097151).astype(jnp.int32)
    control_qubits = set_ends(jax.random.randint(key_list[3], (LAYERS, 4), 0, NQUBITS), jax.random.fold_in(key_list[3], 1), 0, NQUBITS - 1).astype(jnp.int32)
    final_angles = jnp.clip(jax.random.uniform(key_list[4], (QB_BITS,), jnp.float32, -3.140625, 3.140625), -3.140625, 3.140625)
    return {"amplitudes": amplitudes, "gate_angles": gate_angles, "pair_masks": pair_masks, "control_qubits": control_qubits, "final_angles": final_angles}


def pair_lists():
    first_list = []
    second_list = []
    for left in range(7):
        for right in range(left + 1, 7):
            first_list.append(left)
            second_list.append(right)
    return np.array(first_list, np.int32), np.array(second_list, np.int32)


def joined_gate(angles, mask):
    index = jnp.arange(128, dtype=jnp.int32)
    places = jnp.arange(7, dtype=jnp.int32)
    bits = jnp.right_shift(index[:, None], places[None, :]) & 1
    cosine = jnp.cos(angles * 0.5)
    sine = jnp.sin(angles * 0.5)
    rows = bits[:, None, :]
    cols = bits[None, :, :]
    entry = jnp.where(rows == cols, cosine, jnp.where(rows > cols, sine, -sine))
    kron = jnp.prod(entry, axis=2)
    first_list, second_list = pair_lists()
    chosen = jnp.right_shift(mask, jnp.arange(21, dtype=jnp.int32)) & 1
    parity = jnp.sum(chosen[None, :] * bits[:, first_list] * bits[:, second_list], axis=1)
    sign = 1.0 - 2.0 * (parity % 2).astype(jnp.float32)
    return sign[:, None] * kron


def apply_gate(vector, matrix, start, total):
    shaped = vector.reshape(2 ** (total - 7 - start), 128, 2 ** start)
    result = jnp.einsum("ij,ajb->aib", matrix, shaped, precision=lax.Precision.HIGHEST)
    return result.reshape(-1)


def reference(amplitudes, gate_angles, pair_masks, control_qubits, final_angles):
    total = NQUBITS
    vector = amplitudes.reshape(-1)
    starts = [0, 7, LOCAL_QUBITS - 7, total - 7]
    position = jnp.arange(2 ** total, dtype=jnp.int32)
    for layer in range(LAYERS):
        parity = jnp.zeros((2 ** total,), jnp.int32)
        for gate in range(4):
            own_bit = jnp.right_shift(position, starts[gate]) & 1
            ctrl_bit = jnp.right_shift(position, control_qubits[layer, gate]) & 1
            parity = parity + own_bit * ctrl_bit
        vector = vector * (1.0 - 2.0 * (parity % 2).astype(jnp.float32))
        for gate in range(4):
            matrix = joined_gate(gate_angles[layer, gate], pair_masks[layer, gate])
            vector = apply_gate(vector, matrix, starts[gate], total)
    for bit in range(QB_BITS):
        qubit = LOCAL_QUBITS + bit
        cosine = jnp.cos(final_angles[bit] * 0.5)
        sine = jnp.sin(final_angles[bit] * 0.5)
        shaped = vector.reshape(2 ** (total - 1 - qubit), 2, 2 ** qubit)
        lower = shaped[:, 0, :]
        upper = shaped[:, 1, :]
        vector = jnp.stack([cosine * lower - sine * upper, sine * lower + cosine * upper], axis=1).reshape(-1)
    return vector.reshape(amplitudes.shape)
```

```python
import functools
import jax
import jax.numpy as jnp
import numpy as np
from jax import lax
from jax.sharding import PartitionSpec as P
from jax.experimental import pallas as pl
from jax.experimental.pallas import tpu as pltpu

MESH = pl.DeviceIdType.MESH
HI = lax.Precision.HIGHEST


def pair_lists():
    first_list = []
    second_list = []
    for left in range(7):
        for right in range(left + 1, 7):
            first_list.append(left)
            second_list.append(right)
    return (np.array(first_list, np.int32), np.array(second_list, np.int32))


def joined_gate(angles, mask):
    index = jnp.arange(128, dtype=jnp.int32)
    places = jnp.arange(7, dtype=jnp.int32)
    bits = jnp.right_shift(index[:, None], places[None, :]) & 1
    cosine = jnp.cos(angles * 0.5)
    sine = jnp.sin(angles * 0.5)
    rows = bits[:, None, :]
    cols = bits[None, :, :]
    entry = jnp.where(rows == cols, cosine, jnp.where(rows > cols, sine, -sine))
    kron = jnp.prod(entry, axis=2)
    first_list, second_list = pair_lists()
    chosen = jnp.right_shift(mask, jnp.arange(21, dtype=jnp.int32)) & 1
    parity = jnp.sum(chosen[None, :] * bits[:, first_list] * bits[:, second_list], axis=1)
    sign = 1.0 - 2.0 * (parity % 2).astype(jnp.float32)
    return sign[:, None] * kron


def closing(angles):
    index = jnp.arange(128, dtype=jnp.int32)
    places = jnp.arange(4, dtype=jnp.int32)
    bits = jnp.right_shift(index[:, None], places[None, :]) & 1
    cosine = jnp.cos(angles * 0.5)
    sine = jnp.sin(angles * 0.5)
    rows = bits[:, None, :]
    cols = bits[None, :, :]
    entry = jnp.where(rows == cols, cosine, jnp.where(rows > cols, sine, -sine))
    same = (index[:, None] // 16 == index[None, :] // 16).astype(jnp.float32)
    return jnp.prod(entry, axis=2) * same


def a2a_kernel(x_ref, o_ref, send_sem, recv_sem, own_sem):
    qa = lax.axis_index("qa")
    qb = lax.axis_index("qb")
    me = qa * 16 + qb
    x, zh, y, zl, c = qa // 2, qa % 2, qb // 4, (qb // 2) % 2, qb % 2
    z = zh * 2 + zl

    def target(step):
        tc = (c + step % 2) % 2
        tz = (z + (step // 2) % 4) % 4
        ty = (y + (step // 8) % 4) % 4
        tx = (x + step // 32) % 4
        ta = tx * 2 + tz // 2
        tb = ty * 4 + (tz % 2) * 2 + tc
        return ta, tb, ta * 16 + tb

    barrier = pltpu.get_barrier_semaphore()

    def greet(step, carry):
        ta, tb, _ = target(step)
        pl.semaphore_signal(barrier, inc=1, device_id=(ta, tb), device_id_type=MESH)
        return carry

    lax.fori_loop(1, 128, greet, 0)
    own = pltpu.make_async_copy(x_ref.at[me], o_ref.at[me], own_sem)
    own.start()
    pl.semaphore_wait(barrier, 127)

    def send(step, carry):
        ta, tb, index = target((step * 37) % 128)
        pltpu.make_async_remote_copy(
            x_ref.at[index], o_ref.at[me], send_sem, recv_sem,
            device_id=(ta, tb), device_id_type=MESH,
        ).start()
        return carry

    lax.fori_loop(1, 128, send, 0)
    own.wait()
    block = x_ref.at[pl.ds(0, 127)]
    pltpu.make_async_copy(block, block, send_sem).wait()
    pltpu.make_async_copy(block, block, recv_sem).wait()


def exchange(block):
    return pl.pallas_call(
        a2a_kernel,
        out_shape=jax.ShapeDtypeStruct((128, 16, 128), jnp.float32),
        in_specs=[pl.BlockSpec(memory_space=pltpu.VMEM)],
        out_specs=pl.BlockSpec(memory_space=pltpu.VMEM),
        scratch_shapes=[pltpu.SemaphoreType.DMA] * 3,
        compiler_params=pltpu.CompilerParams(collective_id=0, has_side_effects=True),
        name="exchange",
    )(block)


def shards(amplitudes, gate_angles, pair_masks, control_qubits, final_angles):
    device = lax.axis_index("qa") * 16 + lax.axis_index("qb")
    starts = [0, 7, 11, 18]

    def signs(layer, position):
        parity = jnp.zeros(position.shape, jnp.int32)
        for gate in range(4):
            own_bit = jnp.right_shift(position, starts[gate]) & 1
            ctrl_bit = jnp.right_shift(position, control_qubits[layer, gate]) & 1
            parity = parity + own_bit * ctrl_bit
        return 1.0 - 2.0 * (parity % 2).astype(jnp.float32)

    gates = [[joined_gate(gate_angles[l, g], pair_masks[l, g]) for g in range(4)] for l in range(2)]
    low = jnp.arange(2048, dtype=jnp.int32).reshape(16, 128)
    slot = jnp.arange(128, dtype=jnp.int32)[:, None, None]
    vector = amplitudes.reshape(128, 16, 128)
    vector = vector * signs(0, device * 262144 + slot * 2048 + low)
    def local(layer, vector):
        mixed = jnp.einsum("ij,ajb->aib", gates[layer][1], vector.reshape(16, 128, 128), precision=HI)
        return jnp.dot(gates[layer][2], mixed.reshape(128, 2048), precision=HI).reshape(128, 16, 128)

    vector = exchange(local(0, vector))
    vector = jnp.dot(gates[0][3], vector.reshape(128, 2048), precision=HI).reshape(2048, 128)
    vector = jnp.dot(vector, gates[0][0].T, precision=HI)
    vector = vector.reshape(128, 16, 128) * signs(1, slot * 262144 + device * 2048 + low)
    top = jnp.dot(closing(final_angles), gates[1][3], precision=HI)
    vector = jnp.dot(top, vector.reshape(128, 2048), precision=HI).reshape(2048, 128)
    vector = jnp.dot(vector, gates[1][0].T, precision=HI)
    vector = exchange(vector.reshape(128, 16, 128))
    return local(1, vector).reshape(amplitudes.shape)


def solution(mesh):
    return jax.shard_map(
        shards,
        mesh=mesh,
        in_specs=(P("qa", "qb", None), P(), P(), P(), P()),
        out_specs=P("qa", "qb", None),
        check_vma=False,
    )
```

```python
import jax
import jax.numpy as jnp
from jax import lax
from jax.sharding import PartitionSpec as P
from jax.experimental import pallas as pl
from jax.experimental.pallas import tpu as pltpu

F32 = jnp.float32
BF16 = jnp.bfloat16
NATURAL = (0, 1, 2, 3, 4, 5, 6)
MOVED = (6, 3, 4, 5, 0, 1, 2)
STARTS = (0, 7, 11, 18)


def iota(shape, dim):
    return lax.broadcasted_iota(jnp.int32, shape, dim)


def halves(value):
    high = value.astype(BF16)
    return high, (value - high.astype(F32)).astype(BF16)


def gate_parity(index, places, mask):
    bits = [index >> places[j] for j in range(7)]
    parity = None
    pair = 0
    for j in range(6):
        inner = None
        for k in range(j + 1, 7):
            term = (mask >> pair) & bits[k]
            inner = term if inner is None else inner ^ term
            pair += 1
        term = inner & bits[j]
        parity = term if parity is None else parity ^ term
    return parity & 1


def kron_rows(cosine, sine, row_places, col_places, flip):
    lane = iota((1, 128), 1)
    zero, one = [], []
    for j in range(7):
        bit = ((lane >> col_places[j]) & 1) == 1
        low, up = (sine[j], -sine[j]) if flip else (-sine[j], sine[j])
        zero.append(jnp.where(bit, low, cosine[j]))
        one.append(jnp.where(bit, cosine[j], up))
    at = [row_places.index(place) for place in range(7)]
    sub = iota((8, 128), 0)
    value = None
    for place in range(3):
        j = at[place]
        factor = jnp.where(((sub >> place) & 1) == 1, one[j], zero[j])
        value = factor if value is None else value * factor
    for place in range(3, 7):
        j = at[place]
        value = jnp.concatenate([value * zero[j], value * one[j]], axis=0)
    return value


def closing_rows(cosine, sine):
    lane = iota((128, 128), 1)
    row = iota((128, 128), 0)
    value = jnp.where((row >> 4) == (lane >> 4), 1.0, 0.0)
    for j in range(4):
        up = (row >> j) & 1
        across = (lane >> j) & 1
        value = value * jnp.where(up == across, cosine[j], jnp.where(up > across, sine[j], -sine[j]))
    return value


def row_gate(left, value):
    high, low = halves(value)
    out = jnp.dot(left, jnp.concatenate([high, low], axis=0), preferred_element_type=F32)
    return out[:128] + out[128:]


def lane_gate(right, value):
    high, low = halves(value)
    out = jnp.dot(jnp.concatenate([high, low], axis=1), right, preferred_element_type=F32)
    return out[:, :128] + out[:, 128:]


def store_row_matrix(ref, slot, matrix):
    high, low = halves(matrix)
    ref[slot] = jnp.concatenate(
        [jnp.concatenate([high, high], axis=1), jnp.concatenate([low, low], axis=1)], axis=0
    )


def store_lane_matrix(ref, slot, matrix):
    high, low = halves(matrix)
    both = jnp.concatenate([high, low], axis=1)
    ref[slot] = jnp.concatenate([both, both], axis=0)


def kernel(
    x_hbm, angles, masks, controls, final, out_hbm,
    x_v, mid, send1, recv1, send2, recv2, signs, row_mats, lane_mats,
    in_sem, own_sem, send_sem, recv_sem,
):
    qa = lax.axis_index("qa")
    qb = lax.axis_index("qb")
    me = qa * 16 + qb
    load = pltpu.make_async_copy(x_hbm, x_v, in_sem)
    load.start()

    x, zh = lax.div(qa, 2), lax.rem(qa, 2)
    y, zl, core = lax.div(qb, 4), lax.rem(lax.div(qb, 2), 2), lax.rem(qb, 2)
    z = zh * 2 + zl
    near = []
    for dz in (2, 1, 3, 0):
        tz = lax.rem(z + dz, 4)
        for dc in (1, 0):
            tc = lax.rem(core + dc, 2)
            near.append(lax.div(tz, 2) * 16 + lax.rem(tz, 2) * 2 + tc)

    def everyone(action):
        def far(step, carry):
            base = lax.rem(x + lax.div(step, 4) + 2, 4) * 32 + lax.rem(y + lax.rem(step, 4) + 2, 4) * 4
            for other in near:
                action(base + other)
            return carry

        lax.fori_loop(0, 10, far, 0)
        lax.fori_loop(11, 16, far, 0)
        for other in near[:7]:
            action(x * 32 + y * 4 + other)

    barrier = pltpu.get_barrier_semaphore()
    everyone(lambda target: pl.semaphore_signal(
        barrier, inc=1, device_id=target, device_id_type=pl.DeviceIdType.LOGICAL))

    lane1 = iota((1, 128), 1)
    mask_lanes = jnp.zeros((1, 128), jnp.int32)
    for layer in range(2):
        for gate in range(4):
            mask_lanes = jnp.where(lane1 == layer * 4 + gate, masks[layer, gate], mask_lanes)
    row = iota((128, 128), 0)
    sign_nat = 1.0 - 2.0 * gate_parity(row, NATURAL, mask_lanes).astype(F32)
    sign_mov = 1.0 - 2.0 * gate_parity(row, MOVED, mask_lanes).astype(F32)
    cos_all = [jnp.cos(angles[layer] * 0.5) for layer in range(2)]
    sin_all = [jnp.sin(angles[layer] * 0.5) for layer in range(2)]

    def splats(table, gate):
        return [jnp.broadcast_to(table[gate:gate + 1, j:j + 1], (1, 128)) for j in range(7)]

    def row_matrix(layer, gate, row_places, col_places):
        value = kron_rows(splats(cos_all[layer], gate), splats(sin_all[layer], gate), row_places, col_places, False)
        sign = sign_nat if row_places is NATURAL else sign_mov
        column = layer * 4 + gate
        return value * sign[:, column:column + 1]

    def lane_matrix(layer):
        value = kron_rows(splats(cos_all[layer], 0), splats(sin_all[layer], 0), NATURAL, NATURAL, True)
        return value * (1.0 - 2.0 * gate_parity(lane1, NATURAL, masks[layer, 0]).astype(F32))

    def parity_at(layer, position):
        parity = None
        for gate in range(4):
            term = (position >> STARTS[gate]) & (position >> controls[layer, gate])
            parity = term if parity is None else parity ^ term
        return parity & 1

    store_row_matrix(row_mats, 0, row_matrix(0, 1, MOVED, NATURAL))
    store_row_matrix(row_mats, 1, row_matrix(0, 2, NATURAL, NATURAL))
    load.wait()

    spot = row * 128 + iota((128, 128), 1) + me * 262144

    def first_gate(pair, carry):
        blocks = []
        for i in range(2):
            a = pair * 2 + i
            value = x_v[pl.ds(pl.multiple_of(a * 128, 128), 128), :]
            blocks.append(jnp.where(parity_at(0, spot + a * 16384) == 1, -value, value))
        out = row_gate(row_mats[0], jnp.concatenate(blocks, axis=1))
        for i in range(2):
            at = pl.multiple_of((pair * 2 + i) * 8, 8)
            mid[:, pl.ds(at, 8), :] = out[:, i * 128:(i + 1) * 128].reshape(16, 8, 128)
        return carry

    lax.fori_loop(0, 8, first_gate, 0)

    def second_gate(pair, carry):
        kk = pair * 2
        out = row_gate(row_mats[1], jnp.concatenate([mid[kk], mid[kk + 1]], axis=1))
        for i in range(2):
            chunk, group = lax.div(kk + i, 8), lax.rem(kk + i, 8)
            part = out[:, i * 128:(i + 1) * 128].reshape(16, 8, 128)
            for a in range(16):
                send1[chunk, pl.ds(pl.multiple_of((a * 8 + group) * 8, 8), 8), :] = part[a]
        return carry

    lax.fori_loop(0, 8, second_gate, 0)
    pl.semaphore_wait(barrier, 127)

    def rows_of(device):
        return pl.ds(pl.multiple_of(device * 8, 8), 8)

    def ship(stage, chunk, source, landing):
        slot = stage * 2 + chunk
        own = pltpu.make_async_copy(
            source.at[chunk, rows_of(me)], landing.at[chunk, rows_of(me)], own_sem.at[slot])
        own.start()
        everyone(lambda target: pltpu.make_async_remote_copy(
            source.at[chunk, rows_of(target)], landing.at[chunk, rows_of(me)],
            send_sem.at[slot], recv_sem.at[slot],
            device_id=target, device_id_type=pl.DeviceIdType.LOGICAL).start())

    def landed(stage, chunk, source, landing):
        slot = stage * 2 + chunk
        pltpu.make_async_copy(
            source.at[chunk, rows_of(me)], landing.at[chunk, rows_of(me)], own_sem.at[slot]).wait()
        others = landing.at[chunk, pl.ds(0, 127 * 8)]
        pltpu.make_async_copy(others, others, recv_sem.at[slot]).wait()

    ship(0, 0, send1, recv1)
    ship(0, 1, send1, recv1)

    store_row_matrix(row_mats, 2, row_matrix(0, 3, NATURAL, NATURAL))
    store_lane_matrix(lane_mats, 0, lane_matrix(0))
    store_lane_matrix(lane_mats, 1, lane_matrix(1))
    final_half = jnp.zeros((1, 128), F32)
    for j in range(4):
        final_half = jnp.where(lane1 == j, final[j] * 0.5, final_half)
    final_cos, final_sin = jnp.cos(final_half), jnp.sin(final_half)
    closing = closing_rows(
        [jnp.broadcast_to(final_cos[:, j:j + 1], (1, 128)) for j in range(4)],
        [jnp.broadcast_to(final_sin[:, j:j + 1], (1, 128)) for j in range(4)])
    store_row_matrix(row_mats, 6, closing)
    top = row_matrix(1, 3, NATURAL, NATURAL)
    store_row_matrix(row_mats, 3, row_gate(row_mats[6], jnp.concatenate([top, top], axis=1))[:, :128])
    store_row_matrix(row_mats, 4, row_matrix(1, 1, MOVED, MOVED))
    store_row_matrix(row_mats, 5, row_matrix(1, 2, NATURAL, NATURAL))
    here = lax.rem(me, 8) * 256 + lax.div(me, 8) * 16384
    device_spot = row * 262144 + iota((128, 128), 1) + here

    def layer_signs(block, carry):
        spots = device_spot + (lax.div(block, 8) * 128 + lax.rem(block, 8) * 2048)
        signs[block] = jnp.where(parity_at(1, spots) == 1, -1.0, 1.0)
        return carry

    lax.fori_loop(0, 16, layer_signs, 0)

    for chunk in range(2):
        landed(0, chunk, send1, recv1)
        for m in range(0, 8, 2):
            value = jnp.concatenate(
                [recv1[chunk, pl.ds(m + i, 128, stride=8), :] for i in range(2)], axis=1)
            value = row_gate(row_mats[2], value)
            value = jnp.concatenate([value[:, :128], value[:, 128:]], axis=0)
            value = lane_gate(lane_mats[0], value)
            block = chunk * 8 + m
            value = value * jnp.concatenate([signs[block], signs[block + 1]], axis=0)
            value = lane_gate(lane_mats[1], value)
            value = jnp.concatenate([value[:128], value[128:]], axis=1)
            value = row_gate(row_mats[3], value)
            for i in range(2):
                send2[chunk, pl.ds(m + i, 128, stride=8), :] = value[:, i * 128:(i + 1) * 128]
        ship(1, chunk, send2, recv2)

    for chunk in range(2):
        landed(1, chunk, send2, recv2)

    def third_gate(pair, carry):
        blocks = []
        for i in range(2):
            rows = pl.ds(pl.multiple_of((pair * 2 + i) * 64, 64), 64)
            blocks.append(jnp.concatenate([recv2[0, rows, :], recv2[1, rows, :]], axis=0))
        out = row_gate(row_mats[4], jnp.concatenate(blocks, axis=1))
        for i in range(2):
            at = pl.multiple_of((pair * 2 + i) * 8, 8)
            mid[:, pl.ds(at, 8), :] = out[:, i * 128:(i + 1) * 128].reshape(16, 8, 128)
        return carry

    lax.fori_loop(0, 8, third_gate, 0)
    for kk in range(0, 16, 2):
        out = row_gate(row_mats[5], jnp.concatenate([mid[kk], mid[kk + 1]], axis=1))
        for i in range(2):
            k = (kk + i) // 8 + 2 * ((kk + i) % 8)
            x_v[pl.ds(k, 128, stride=16), :] = out[:, i * 128:(i + 1) * 128]
    store = pltpu.make_async_copy(x_v, out_hbm, in_sem)
    store.start()
    for slot in range(4):
        source = (send1, send2)[slot // 2]
        others = source.at[slot % 2, pl.ds(0, 127 * 8)]
        pltpu.make_async_copy(others, others, send_sem.at[slot]).wait()
    store.wait()


def shards(amplitudes, gate_angles, pair_masks, control_qubits, final_angles):
    out = pl.pallas_call(
        kernel,
        out_shape=jax.ShapeDtypeStruct((2048, 128), F32),
        in_specs=[
            pl.BlockSpec(memory_space=pl.ANY),
            pl.BlockSpec(memory_space=pltpu.VMEM),
            pl.BlockSpec(memory_space=pltpu.SMEM),
            pl.BlockSpec(memory_space=pltpu.SMEM),
            pl.BlockSpec(memory_space=pltpu.SMEM),
        ],
        out_specs=pl.BlockSpec(memory_space=pl.ANY),
        scratch_shapes=[
            pltpu.VMEM((2048, 128), F32),
            pltpu.VMEM((16, 128, 128), F32),
            pltpu.VMEM((2, 1024, 128), F32),
            pltpu.VMEM((2, 1024, 128), F32),
            pltpu.VMEM((2, 1024, 128), F32),
            pltpu.VMEM((2, 1024, 128), F32),
            pltpu.VMEM((16, 128, 128), F32),
            pltpu.VMEM((7, 256, 256), BF16),
            pltpu.VMEM((2, 256, 256), BF16),
            pltpu.SemaphoreType.DMA,
            pltpu.SemaphoreType.DMA((4,)),
            pltpu.SemaphoreType.DMA((4,)),
            pltpu.SemaphoreType.DMA((4,)),
        ],
        compiler_params=pltpu.CompilerParams(
            collective_id=0, has_side_effects=True, vmem_limit_bytes=24 * 2**20),
        name="layers",
    )(amplitudes.reshape(2048, 128), gate_angles, pair_masks, control_qubits, final_angles)
    return out.reshape(amplitudes.shape)


def solution(mesh):
    return jax.shard_map(
        shards,
        mesh=mesh,
        in_specs=(P("qa", "qb", None), P(), P(), P(), P()),
        out_specs=P("qa", "qb", None),
        check_vma=False,
    )
```

```python
import jax
import jax.numpy as jnp
from jax import lax
from jax.sharding import PartitionSpec as P
from jax.experimental import pallas as pl
from jax.experimental.pallas import tpu as pltpu

F32 = jnp.float32
BF16 = jnp.bfloat16
NATURAL = (0, 1, 2, 3, 4, 5, 6)
MOVED = (6, 3, 4, 5, 0, 1, 2)
STARTS = (0, 7, 11, 18)
FAR_FIRST = tuple((dx, dy) for dx in (2, 1, 3, 0) for dy in (2, 1, 3, 0))


def iota(shape, dim):
    return lax.broadcasted_iota(jnp.int32, shape, dim)


def halves(value):
    high = value.astype(BF16)
    return high, (value - high.astype(F32)).astype(BF16)


def gate_parity(index, places, mask):
    bits = [index >> places[j] for j in range(7)]
    parity = None
    pair = 0
    for j in range(6):
        inner = None
        for k in range(j + 1, 7):
            term = (mask >> pair) & bits[k]
            inner = term if inner is None else inner ^ term
            pair += 1
        term = inner & bits[j]
        parity = term if parity is None else parity ^ term
    return parity & 1


def kron_rows(cosine, sine, row_places, col_places, flip):
    lane = iota((1, 128), 1)
    zero, one = [], []
    for j in range(7):
        bit = ((lane >> col_places[j]) & 1) == 1
        low, up = (sine[j], -sine[j]) if flip else (-sine[j], sine[j])
        zero.append(jnp.where(bit, low, cosine[j]))
        one.append(jnp.where(bit, cosine[j], up))
    at = [row_places.index(place) for place in range(7)]
    sub = iota((8, 128), 0)
    value = None
    for place in range(3):
        j = at[place]
        factor = jnp.where(((sub >> place) & 1) == 1, one[j], zero[j])
        value = factor if value is None else value * factor
    for place in range(3, 7):
        j = at[place]
        value = jnp.concatenate([value * zero[j], value * one[j]], axis=0)
    return value


def closing_rows(cosine, sine):
    lane = iota((128, 128), 1)
    row = iota((128, 128), 0)
    value = jnp.where((row >> 4) == (lane >> 4), 1.0, 0.0)
    for j in range(4):
        up = (row >> j) & 1
        across = (lane >> j) & 1
        value = value * jnp.where(up == across, cosine[j], jnp.where(up > across, sine[j], -sine[j]))
    return value


def row_gate(left, value):
    high, low = halves(value)
    out = jnp.dot(left, jnp.concatenate([high, low], axis=0), preferred_element_type=F32)
    return out[:128] + out[128:]


def lane_gate(right, value):
    high, low = halves(value)
    out = jnp.dot(jnp.concatenate([high, low], axis=1), right, preferred_element_type=F32)
    return out[:, :128] + out[:, 128:]


def store_row_matrix(ref, slot, matrix):
    high, low = halves(matrix)
    ref[slot] = jnp.concatenate(
        [jnp.concatenate([high, high], axis=1), jnp.concatenate([low, low], axis=1)], axis=0
    )


def store_lane_matrix(ref, slot, matrix):
    high, low = halves(matrix)
    both = jnp.concatenate([high, low], axis=1)
    ref[slot] = jnp.concatenate([both, both], axis=0)


def kernel(
    x_hbm, angles_hbm, masks_hbm, controls_hbm, final_hbm, out,
    x_v, angles, masks, controls, final,
    mid, send1, recv1, send2, recv2, signs, row_mats, lane_mats,
    in_sem, own_sem, send_sem, recv_sem,
):
    qa = lax.axis_index("qa")
    qb = lax.axis_index("qb")
    me = qa * 16 + qb
    loads = [
        pltpu.make_async_copy(source, place, in_sem.at[slot])
        for slot, (source, place) in enumerate((
            (angles_hbm, angles), (masks_hbm, masks), (controls_hbm, controls),
            (final_hbm, final), (x_hbm, x_v)))
    ]
    for load in loads:
        load.start()

    x, zh = lax.div(qa, 2), lax.rem(qa, 2)
    y, zl, core = lax.div(qb, 4), lax.rem(lax.div(qb, 2), 2), lax.rem(qb, 2)
    z = zh * 2 + zl
    near = []
    for dz in (2, 1, 3, 0):
        tz = lax.rem(z + dz, 4)
        for dc in (1, 0):
            tc = lax.rem(core + dc, 2)
            near.append(lax.div(tz, 2) * 16 + lax.rem(tz, 2) * 2 + tc)

    def everyone(action):
        def far(step, carry):
            base = lax.rem(x + lax.div(step, 4) + 2, 4) * 32 + lax.rem(y + lax.rem(step, 4) + 2, 4) * 4
            for other in near:
                action(base + other)
            return carry

        lax.fori_loop(0, 10, far, 0)
        lax.fori_loop(11, 16, far, 0)
        for other in near[:7]:
            action(x * 32 + y * 4 + other)

    barrier = pltpu.get_barrier_semaphore()
    columns = [lax.rem(x + dx, 4) * 32 for dx in range(4)]
    lines = [lax.rem(y + dy, 4) * 4 for dy in range(4)]
    for dx, dy in FAR_FIRST:
        base = columns[dx] + lines[dy]
        for other in near if (dx, dy) != (0, 0) else near[:7]:
            pl.semaphore_signal(
                barrier, inc=1, device_id=base + other, device_id_type=pl.DeviceIdType.LOGICAL)
    for load in loads[:4]:
        load.wait()

    lane1 = iota((1, 128), 1)
    mask_lanes = jnp.zeros((1, 128), jnp.int32)
    for layer in range(2):
        for gate in range(4):
            mask_lanes = jnp.where(lane1 == layer * 4 + gate, masks[layer, gate], mask_lanes)
    row = iota((128, 128), 0)
    sign_nat = 1.0 - 2.0 * gate_parity(row, NATURAL, mask_lanes).astype(F32)
    sign_mov = 1.0 - 2.0 * gate_parity(row, MOVED, mask_lanes).astype(F32)
    cos_all = [jnp.cos(angles[layer] * 0.5) for layer in range(2)]
    sin_all = [jnp.sin(angles[layer] * 0.5) for layer in range(2)]

    def splats(table, gate):
        return [jnp.broadcast_to(table[gate:gate + 1, j:j + 1], (1, 128)) for j in range(7)]

    def row_matrix(layer, gate, row_places, col_places):
        value = kron_rows(splats(cos_all[layer], gate), splats(sin_all[layer], gate), row_places, col_places, False)
        sign = sign_nat if row_places is NATURAL else sign_mov
        column = layer * 4 + gate
        return value * sign[:, column:column + 1]

    def lane_matrix(layer):
        value = kron_rows(splats(cos_all[layer], 0), splats(sin_all[layer], 0), NATURAL, NATURAL, True)
        return value * (1.0 - 2.0 * gate_parity(lane1, NATURAL, masks[layer, 0]).astype(F32))

    def parity_at(layer, position):
        parity = None
        for gate in range(4):
            term = (position >> STARTS[gate]) & (position >> controls[layer, gate])
            parity = term if parity is None else parity ^ term
        return parity & 1

    store_row_matrix(row_mats, 0, row_matrix(0, 1, MOVED, NATURAL))
    store_row_matrix(row_mats, 1, row_matrix(0, 2, NATURAL, NATURAL))
    lanes8, sub8 = iota((8, 128), 1), iota((8, 128), 0)
    column = iota((128, 128), 1)
    parity = parity_at(0, row * 128 + column + me * 262144)
    first_signs = jnp.where(parity == 1, -1.0, 1.0)
    loads[4].wait()
    for pair in range(8):
        blocks = []
        for i in range(2):
            a = pair * 2 + i
            bits = [((a * 16384) >> controls[0, gate]) & 1 for gate in range(4)]
            flip = (bits[0] & lanes8) ^ (bits[1] & sub8) ^ (bits[3] & core)
            even = jnp.where((flip & 1) == 1, -1.0, 1.0)
            odd = jnp.where(((flip ^ bits[2]) & 1) == 1, -1.0, 1.0)
            factor = jnp.concatenate([even, even, odd, odd] * 4, axis=0)
            blocks.append(x_v[a * 128:(a + 1) * 128, :] * first_signs * factor)
        out_pair = row_gate(row_mats[0], jnp.concatenate(blocks, axis=1))
        for i in range(2):
            a = pair * 2 + i
            mid[:, a * 8:(a + 1) * 8, :] = out_pair[:, i * 128:(i + 1) * 128].reshape(16, 8, 128)

    def second_gate(chunk):
        for group in range(0, 8, 2):
            kk = chunk * 8 + group
            mixed = row_gate(row_mats[1], jnp.concatenate([mid[kk], mid[kk + 1]], axis=1))
            for i in range(2):
                part = mixed[:, i * 128:(i + 1) * 128].reshape(16, 8, 128)
                for a in range(16):
                    at = (a * 8 + group + i) * 8
                    send1[chunk, at:at + 8, :] = part[a]

    def rows_of(device):
        return pl.ds(pl.multiple_of(device * 8, 8), 8)

    def ship(stage, chunk, source, landing):
        slot = stage * 2 + chunk
        own = pltpu.make_async_copy(
            source.at[chunk, rows_of(me)], landing.at[chunk, rows_of(me)], own_sem.at[slot])
        own.start()
        everyone(lambda target: pltpu.make_async_remote_copy(
            source.at[chunk, rows_of(target)], landing.at[chunk, rows_of(me)],
            send_sem.at[slot], recv_sem.at[slot],
            device_id=target, device_id_type=pl.DeviceIdType.LOGICAL).start())

    def landed(stage, chunk, source, landing):
        slot = stage * 2 + chunk
        pltpu.make_async_copy(
            source.at[chunk, rows_of(me)], landing.at[chunk, rows_of(me)], own_sem.at[slot]).wait()
        others = landing.at[chunk, pl.ds(0, 127 * 8)]
        pltpu.make_async_copy(others, others, recv_sem.at[slot]).wait()

    second_gate(0)
    pl.semaphore_wait(barrier, 127)
    ship(0, 0, send1, recv1)
    second_gate(1)
    ship(0, 1, send1, recv1)

    store_row_matrix(row_mats, 2, row_matrix(0, 3, NATURAL, NATURAL))
    store_lane_matrix(lane_mats, 0, lane_matrix(0))
    store_lane_matrix(lane_mats, 1, lane_matrix(1))
    final_half = jnp.zeros((1, 128), F32)
    for j in range(4):
        final_half = jnp.where(lane1 == j, final[j] * 0.5, final_half)
    final_cos, final_sin = jnp.cos(final_half), jnp.sin(final_half)
    closing = closing_rows(
        [jnp.broadcast_to(final_cos[:, j:j + 1], (1, 128)) for j in range(4)],
        [jnp.broadcast_to(final_sin[:, j:j + 1], (1, 128)) for j in range(4)])
    store_row_matrix(row_mats, 6, closing)
    top = row_matrix(1, 3, NATURAL, NATURAL)
    store_row_matrix(row_mats, 3, row_gate(row_mats[6], jnp.concatenate([top, top], axis=1))[:, :128])
    store_row_matrix(row_mats, 4, row_matrix(1, 1, MOVED, MOVED))
    store_row_matrix(row_mats, 5, row_matrix(1, 2, NATURAL, NATURAL))
    here = lax.rem(me, 8) * 256 + lax.div(me, 8) * 16384
    device_spot = row * 262144 + iota((128, 128), 1) + here

    def layer_signs(block, carry):
        spots = device_spot + (lax.div(block, 8) * 128 + lax.rem(block, 8) * 2048)
        signs[block] = jnp.where(parity_at(1, spots) == 1, -1.0, 1.0)
        return carry

    lax.fori_loop(0, 16, layer_signs, 0)

    for chunk in range(2):
        landed(0, chunk, send1, recv1)
        for m in range(0, 8, 2):
            value = jnp.concatenate(
                [recv1[chunk, pl.ds(m + i, 128, stride=8), :] for i in range(2)], axis=1)
            value = row_gate(row_mats[2], value)
            value = jnp.concatenate([value[:, :128], value[:, 128:]], axis=0)
            value = lane_gate(lane_mats[0], value)
            block = chunk * 8 + m
            value = value * jnp.concatenate([signs[block], signs[block + 1]], axis=0)
            value = lane_gate(lane_mats[1], value)
            value = jnp.concatenate([value[:128], value[128:]], axis=1)
            value = row_gate(row_mats[3], value)
            for i in range(2):
                send2[chunk, pl.ds(m + i, 128, stride=8), :] = value[:, i * 128:(i + 1) * 128]
        ship(1, chunk, send2, recv2)

    for chunk in range(2):
        landed(1, chunk, send2, recv2)

    for pair in range(8):
        blocks = []
        for i in range(2):
            at = (pair * 2 + i) * 64
            blocks.append(jnp.concatenate([recv2[0, at:at + 64, :], recv2[1, at:at + 64, :]], axis=0))
        out_pair = row_gate(row_mats[4], jnp.concatenate(blocks, axis=1))
        for i in range(2):
            a = pair * 2 + i
            mid[:, a * 8:(a + 1) * 8, :] = out_pair[:, i * 128:(i + 1) * 128].reshape(16, 8, 128)
    for kk in range(0, 16, 2):
        mixed = row_gate(row_mats[5], jnp.concatenate([mid[kk], mid[kk + 1]], axis=1))
        for i in range(2):
            k = (kk + i) // 8 + 2 * ((kk + i) % 8)
            out[pl.ds(k, 128, stride=16), :] = mixed[:, i * 128:(i + 1) * 128]
    for slot in range(4):
        source = (send1, send2)[slot // 2]
        others = source.at[slot % 2, pl.ds(0, 127 * 8)]
        pltpu.make_async_copy(others, others, send_sem.at[slot]).wait()


def shards(amplitudes, gate_angles, pair_masks, control_qubits, final_angles):
    out = pl.pallas_call(
        kernel,
        out_shape=jax.ShapeDtypeStruct((2048, 128), F32),
        in_specs=[pl.BlockSpec(memory_space=pltpu.HBM)] * 5,
        out_specs=pl.BlockSpec(memory_space=pltpu.VMEM),
        scratch_shapes=[
            pltpu.VMEM((2048, 128), F32),
            pltpu.VMEM(gate_angles.shape, F32),
            pltpu.SMEM(pair_masks.shape, jnp.int32),
            pltpu.SMEM(control_qubits.shape, jnp.int32),
            pltpu.SMEM(final_angles.shape, F32),
            pltpu.VMEM((16, 128, 128), F32),
            pltpu.VMEM((2, 1024, 128), F32),
            pltpu.VMEM((2, 1024, 128), F32),
            pltpu.VMEM((2, 1024, 128), F32),
            pltpu.VMEM((2, 1024, 128), F32),
            pltpu.VMEM((16, 128, 128), F32),
            pltpu.VMEM((7, 256, 256), BF16),
            pltpu.VMEM((2, 256, 256), BF16),
            pltpu.SemaphoreType.DMA((5,)),
            pltpu.SemaphoreType.DMA((4,)),
            pltpu.SemaphoreType.DMA((4,)),
            pltpu.SemaphoreType.DMA((4,)),
        ],
        compiler_params=pltpu.CompilerParams(
            collective_id=0, has_side_effects=True, vmem_limit_bytes=24 * 2**20),
        name="layers",
    )(*(pltpu.with_memory_space_constraint(value, pltpu.HBM) for value in (
        amplitudes.reshape(2048, 128), gate_angles, pair_masks, control_qubits, final_angles)))
    return out.reshape(amplitudes.shape)


def solution(mesh):
    return jax.shard_map(
        shards,
        mesh=mesh,
        in_specs=(P("qa", "qb", None), P(), P(), P(), P()),
        out_specs=P("qa", "qb", None),
        check_vma=False,
    )
```

```python
import jax
import jax.numpy as jnp
from jax import lax
from jax.sharding import PartitionSpec as P
from jax.experimental import pallas as pl
from jax.experimental.pallas import tpu as pltpu

F32 = jnp.float32
BF16 = jnp.bfloat16
NATURAL = (0, 1, 2, 3, 4, 5, 6)
MOVED = (6, 3, 4, 5, 0, 1, 2)
STARTS = (0, 7, 11, 18)
STEPS = [(n // 32, n // 8 % 4, n // 2 % 4, n % 2) for n in range(1, 128)]
def reach(step):
    return sum(min(part, 4 - part) for part in step[:3])
ORDER = sorted(STEPS, key=lambda step: (-reach(step), (step[0] * 32 + step[1] * 8 + step[2] * 2 + step[3]) * 53 % 128))


def iota(shape, dim):
    return lax.broadcasted_iota(jnp.int32, shape, dim)


def halves(value):
    high = value.astype(BF16)
    return high, (value - high.astype(F32)).astype(BF16)


def gate_parity(index, places, mask):
    bits = [index >> places[j] for j in range(7)]
    parity = None
    pair = 0
    for j in range(6):
        inner = None
        for k in range(j + 1, 7):
            term = (mask >> pair) & bits[k]
            inner = term if inner is None else inner ^ term
            pair += 1
        term = inner & bits[j]
        parity = term if parity is None else parity ^ term
    return parity & 1


def kron_rows(cosine, sine, row_places, col_places, flip):
    lane = iota((1, 128), 1)
    zero, one = [], []
    for j in range(7):
        bit = ((lane >> col_places[j]) & 1) == 1
        low, up = (sine[j], -sine[j]) if flip else (-sine[j], sine[j])
        zero.append(jnp.where(bit, low, cosine[j]))
        one.append(jnp.where(bit, cosine[j], up))
    at = [row_places.index(place) for place in range(7)]
    sub = iota((8, 128), 0)
    value = None
    for place in range(3):
        j = at[place]
        factor = jnp.where(((sub >> place) & 1) == 1, one[j], zero[j])
        value = factor if value is None else value * factor
    for place in range(3, 7):
        j = at[place]
        value = jnp.concatenate([value * zero[j], value * one[j]], axis=0)
    return value


def closing_rows(cosine, sine):
    lane = iota((128, 128), 1)
    row = iota((128, 128), 0)
    value = jnp.where((row >> 4) == (lane >> 4), 1.0, 0.0)
    for j in range(4):
        up = (row >> j) & 1
        across = (lane >> j) & 1
        value = value * jnp.where(up == across, cosine[j], jnp.where(up > across, sine[j], -sine[j]))
    return value


def row_gate(left, value):
    high, low = halves(value)
    out = jnp.dot(left, jnp.concatenate([high, low], axis=0), preferred_element_type=F32)
    return out[:128] + out[128:]


def lane_gate(right, value):
    high, low = halves(value)
    out = jnp.dot(jnp.concatenate([high, low], axis=1), right, preferred_element_type=F32)
    return out[:, :128] + out[:, 128:]


def store_row_matrix(ref, slot, matrix):
    high, low = halves(matrix)
    ref[slot] = jnp.concatenate(
        [jnp.concatenate([high, high], axis=1), jnp.concatenate([low, low], axis=1)], axis=0
    )


def store_lane_matrix(ref, slot, matrix):
    high, low = halves(matrix)
    both = jnp.concatenate([high, low], axis=1)
    ref[slot] = jnp.concatenate([both, both], axis=0)


def kernel(
    x_hbm, angles_hbm, masks_hbm, controls_hbm, final_hbm, out,
    x_v, angles, masks, controls, final,
    mid, send1, recv1, send2, recv2, signs, row_mats, lane_mats,
    in_sem, own_sem, send_sem, recv_sem,
):
    qa = lax.axis_index("qa")
    qb = lax.axis_index("qb")
    me = qa * 16 + qb
    loads = [
        pltpu.make_async_copy(source, place, in_sem.at[slot])
        for slot, (source, place) in enumerate((
            (angles_hbm, angles), (masks_hbm, masks), (controls_hbm, controls),
            (final_hbm, final), (x_hbm, x_v)))
    ]
    for load in loads:
        load.start()

    x, zh = lax.div(qa, 2), lax.rem(qa, 2)
    y, zl, core = lax.div(qb, 4), lax.rem(lax.div(qb, 2), 2), lax.rem(qb, 2)
    z = zh * 2 + zl
    way = 1 - 2 * core
    columns = [lax.rem(x + 4 + way * dx, 4) * 32 for dx in range(4)]
    lines = [lax.rem(y + 4 + way * dy, 4) * 4 for dy in range(4)]
    levels = [lax.rem(z + 4 + way * dz, 4) for dz in range(4)]
    cores = [core, 1 - core]
    inner = [[lax.div(tz, 2) * 16 + lax.rem(tz, 2) * 2 + tc for tc in cores] for tz in levels]
    outer = [[column + line for line in lines] for column in columns]

    def everyone(action):
        for dx, dy, dz, dc in ORDER:
            action(outer[dx][dy] + inner[dz][dc])

    barrier = pltpu.get_barrier_semaphore()
    everyone(lambda target: pl.semaphore_signal(
        barrier, inc=1, device_id=target, device_id_type=pl.DeviceIdType.LOGICAL))
    for load in loads[:4]:
        load.wait()

    lane1 = iota((1, 128), 1)
    mask_lanes = jnp.zeros((1, 128), jnp.int32)
    for layer in range(2):
        for gate in range(4):
            mask_lanes = jnp.where(lane1 == layer * 4 + gate, masks[layer, gate], mask_lanes)
    row = iota((128, 128), 0)
    sign_nat = 1.0 - 2.0 * gate_parity(row, NATURAL, mask_lanes).astype(F32)
    sign_mov = 1.0 - 2.0 * gate_parity(row, MOVED, mask_lanes).astype(F32)
    cos_all = [jnp.cos(angles[layer] * 0.5) for layer in range(2)]
    sin_all = [jnp.sin(angles[layer] * 0.5) for layer in range(2)]

    def splats(table, gate):
        return [jnp.broadcast_to(table[gate:gate + 1, j:j + 1], (1, 128)) for j in range(7)]

    def row_matrix(layer, gate, row_places, col_places):
        value = kron_rows(splats(cos_all[layer], gate), splats(sin_all[layer], gate), row_places, col_places, False)
        sign = sign_nat if row_places is NATURAL else sign_mov
        column = layer * 4 + gate
        return value * sign[:, column:column + 1]

    def lane_matrix(layer):
        value = kron_rows(splats(cos_all[layer], 0), splats(sin_all[layer], 0), NATURAL, NATURAL, True)
        return value * (1.0 - 2.0 * gate_parity(lane1, NATURAL, masks[layer, 0]).astype(F32))

    def parity_at(layer, position):
        parity = None
        for gate in range(4):
            term = (position >> STARTS[gate]) & (position >> controls[layer, gate])
            parity = term if parity is None else parity ^ term
        return parity & 1

    store_lane_matrix(lane_mats, 0, lane_matrix(0))
    store_row_matrix(row_mats, 0, row_matrix(0, 1, MOVED, NATURAL))
    store_row_matrix(row_mats, 1, row_matrix(0, 2, NATURAL, NATURAL))
    lanes8, sub8 = iota((8, 128), 1), iota((8, 128), 0)
    column = iota((128, 128), 1)
    parity = parity_at(0, row * 128 + column + me * 262144)
    first_signs = jnp.where(parity == 1, -1.0, 1.0)
    loads[4].wait()
    for pair in range(8):
        blocks = []
        for i in range(2):
            a = pair * 2 + i
            bits = [((a * 16384) >> controls[0, gate]) & 1 for gate in range(4)]
            flip = (bits[0] & lanes8) ^ (bits[1] & sub8) ^ (bits[3] & core)
            even = jnp.where((flip & 1) == 1, -1.0, 1.0)
            odd = jnp.where(((flip ^ bits[2]) & 1) == 1, -1.0, 1.0)
            factor = jnp.concatenate([even, even, odd, odd] * 4, axis=0)
            blocks.append(x_v[a * 128:(a + 1) * 128, :] * first_signs * factor)
        mixed = lane_gate(lane_mats[0], jnp.concatenate(blocks, axis=0))
        out_pair = row_gate(row_mats[0], jnp.concatenate([mixed[:128], mixed[128:]], axis=1))
        for i in range(2):
            a = pair * 2 + i
            mid[:, a * 8:(a + 1) * 8, :] = out_pair[:, i * 128:(i + 1) * 128].reshape(16, 8, 128)

    def second_gate(chunk):
        for group in range(0, 8, 2):
            kk = chunk * 8 + group
            mixed = row_gate(row_mats[1], jnp.concatenate([mid[kk], mid[kk + 1]], axis=1))
            for i in range(2):
                part = mixed[:, i * 128:(i + 1) * 128].reshape(16, 8, 128)
                for a in range(16):
                    at = (a * 8 + group + i) * 8
                    send1[chunk, at:at + 8, :] = part[a]

    def rows_of(device):
        return pl.ds(pl.multiple_of(device * 8, 8), 8)

    def ship(stage, chunk, source, landing):
        slot = stage * 2 + chunk
        own = pltpu.make_async_copy(
            source.at[chunk, rows_of(me)], landing.at[chunk, rows_of(me)], own_sem.at[slot])
        own.start()
        everyone(lambda target: pltpu.make_async_remote_copy(
            source.at[chunk, rows_of(target)], landing.at[chunk, rows_of(me)],
            send_sem.at[slot], recv_sem.at[slot],
            device_id=target, device_id_type=pl.DeviceIdType.LOGICAL).start())

    def landed(stage, chunk, source, landing):
        slot = stage * 2 + chunk
        pltpu.make_async_copy(
            source.at[chunk, rows_of(me)], landing.at[chunk, rows_of(me)], own_sem.at[slot]).wait()
        others = landing.at[chunk, pl.ds(0, 127 * 8)]
        pltpu.make_async_copy(others, others, recv_sem.at[slot]).wait()

    second_gate(0)
    pl.semaphore_wait(barrier, 127)
    ship(0, 0, send1, recv1)
    second_gate(1)
    ship(0, 1, send1, recv1)

    store_row_matrix(row_mats, 2, row_matrix(0, 3, NATURAL, NATURAL))
    store_lane_matrix(lane_mats, 1, lane_matrix(1))
    final_half = jnp.zeros((1, 128), F32)
    for j in range(4):
        final_half = jnp.where(lane1 == j, final[j] * 0.5, final_half)
    final_cos, final_sin = jnp.cos(final_half), jnp.sin(final_half)
    closing = closing_rows(
        [jnp.broadcast_to(final_cos[:, j:j + 1], (1, 128)) for j in range(4)],
        [jnp.broadcast_to(final_sin[:, j:j + 1], (1, 128)) for j in range(4)])
    store_row_matrix(row_mats, 6, closing)
    top = row_matrix(1, 3, NATURAL, NATURAL)
    store_row_matrix(row_mats, 3, row_gate(row_mats[6], jnp.concatenate([top, top], axis=1))[:, :128])
    store_row_matrix(row_mats, 4, row_matrix(1, 1, MOVED, MOVED))
    store_row_matrix(row_mats, 5, row_matrix(1, 2, NATURAL, NATURAL))
    here = lax.rem(me, 8) * 256 + lax.div(me, 8) * 16384
    device_spot = row * 262144 + iota((128, 128), 1) + here

    def layer_signs(block, carry):
        spots = device_spot + (lax.div(block, 8) * 128 + lax.rem(block, 8) * 2048)
        signs[block] = jnp.where(parity_at(1, spots) == 1, -1.0, 1.0)
        return carry

    lax.fori_loop(0, 16, layer_signs, 0)

    for chunk in range(2):
        landed(0, chunk, send1, recv1)
        values = []
        for m in range(0, 8, 2):
            value = jnp.concatenate(
                [recv1[chunk, pl.ds(m + i, 128, stride=8), :] for i in range(2)], axis=1)
            values.append(row_gate(row_mats[2], value))
        for pair in range(4):
            value, block = values[pair], chunk * 8 + pair * 2
            value = jnp.concatenate(
                [value[:, :128] * signs[block], value[:, 128:] * signs[block + 1]], axis=0)
            value = lane_gate(lane_mats[1], value)
            values[pair] = jnp.concatenate([value[:128], value[128:]], axis=1)
        for pair in range(4):
            value = row_gate(row_mats[3], values[pair])
            for i in range(2):
                send2[chunk, pl.ds(pair * 2 + i, 128, stride=8), :] = value[:, i * 128:(i + 1) * 128]
        ship(1, chunk, send2, recv2)

    for chunk in range(2):
        landed(1, chunk, send2, recv2)

    for pair in range(8):
        blocks = []
        for i in range(2):
            at = (pair * 2 + i) * 64
            blocks.append(jnp.concatenate([recv2[0, at:at + 64, :], recv2[1, at:at + 64, :]], axis=0))
        out_pair = row_gate(row_mats[4], jnp.concatenate(blocks, axis=1))
        for i in range(2):
            a = pair * 2 + i
            mid[:, a * 8:(a + 1) * 8, :] = out_pair[:, i * 128:(i + 1) * 128].reshape(16, 8, 128)
    for kk in range(0, 16, 2):
        mixed = row_gate(row_mats[5], jnp.concatenate([mid[kk], mid[kk + 1]], axis=1))
        for i in range(2):
            k = (kk + i) // 8 + 2 * ((kk + i) % 8)
            out[pl.ds(k, 128, stride=16), :] = mixed[:, i * 128:(i + 1) * 128]
    for slot in range(4):
        source = (send1, send2)[slot // 2]
        others = source.at[slot % 2, pl.ds(0, 127 * 8)]
        pltpu.make_async_copy(others, others, send_sem.at[slot]).wait()


def shards(amplitudes, gate_angles, pair_masks, control_qubits, final_angles):
    out = pl.pallas_call(
        kernel,
        out_shape=jax.ShapeDtypeStruct((2048, 128), F32),
        in_specs=[pl.BlockSpec(memory_space=pltpu.HBM)] * 5,
        out_specs=pl.BlockSpec(memory_space=pltpu.VMEM),
        scratch_shapes=[
            pltpu.VMEM((2048, 128), F32),
            pltpu.VMEM(gate_angles.shape, F32),
            pltpu.SMEM(pair_masks.shape, jnp.int32),
            pltpu.SMEM(control_qubits.shape, jnp.int32),
            pltpu.SMEM(final_angles.shape, F32),
            pltpu.VMEM((16, 128, 128), F32),
            pltpu.VMEM((2, 1024, 128), F32),
            pltpu.VMEM((2, 1024, 128), F32),
            pltpu.VMEM((2, 1024, 128), F32),
            pltpu.VMEM((2, 1024, 128), F32),
            pltpu.VMEM((16, 128, 128), F32),
            pltpu.VMEM((7, 256, 256), BF16),
            pltpu.VMEM((2, 256, 256), BF16),
            pltpu.SemaphoreType.DMA((5,)),
            pltpu.SemaphoreType.DMA((4,)),
            pltpu.SemaphoreType.DMA((4,)),
            pltpu.SemaphoreType.DMA((4,)),
        ],
        compiler_params=pltpu.CompilerParams(
            collective_id=0, has_side_effects=True, vmem_limit_bytes=24 * 2**20),
        name="layers",
    )(*(pltpu.with_memory_space_constraint(value, pltpu.HBM) for value in (
        amplitudes.reshape(2048, 128), gate_angles, pair_masks, control_qubits, final_angles)))
    return out.reshape(amplitudes.shape)


def solution(mesh):
    return jax.shard_map(
        shards,
        mesh=mesh,
        in_specs=(P("qa", "qb", None), P(), P(), P(), P()),
        out_specs=P("qa", "qb", None),
        check_vma=False,
    )
```

```python
import jax
import jax.numpy as jnp
from jax import lax
from jax.sharding import PartitionSpec as P
from jax.experimental import pallas as pl
from jax.experimental.pallas import tpu as pltpu

F32 = jnp.float32
BF16 = jnp.bfloat16
NATURAL = (0, 1, 2, 3, 4, 5, 6)
MOVED = (3, 4, 5, 6, 0, 1, 2)
STARTS = (0, 7, 11, 18)
STEPS = [(n // 32, n // 8 % 4, n // 2 % 4, n % 2) for n in range(1, 128)]


def hops(step):
    return sum(min(part, 4 - part) for part in step[:3])


def spread(step):
    return (step[0] * 32 + step[1] * 8 + step[2] * 2 + step[3]) * 53 % 128


def first_axis(step):
    return 0 if step[0] else 1 if step[1] else 2


def merged(steps):
    placed = []
    for kind in range(3):
        group = [step for step in steps if first_axis(step) == kind]
        placed += [((n + 0.5) / len(group), step) for n, step in enumerate(group)]
    return [step for _, step in sorted(placed)]


FAR_FIRST = sorted(STEPS, key=lambda step: (-hops(step), spread(step)))
SENDS = merged(FAR_FIRST)


def iota(shape, dim):
    return lax.broadcasted_iota(jnp.int32, shape, dim)


def halves(value):
    high = value.astype(BF16)
    return high, (value - high.astype(F32)).astype(BF16)


def gate_parity(index, places, mask):
    bits = [index >> places[j] for j in range(7)]
    parity = None
    pair = 0
    for j in range(6):
        inner = None
        for k in range(j + 1, 7):
            term = (mask >> pair) & bits[k]
            inner = term if inner is None else inner ^ term
            pair += 1
        term = inner & bits[j]
        parity = term if parity is None else parity ^ term
    return parity & 1


def kron_rows(cosine, sine, row_places, col_places, flip):
    lane = iota((1, 128), 1)
    zero, one = [], []
    for j in range(7):
        bit = ((lane >> col_places[j]) & 1) == 1
        low, up = (sine[j], -sine[j]) if flip else (-sine[j], sine[j])
        zero.append(jnp.where(bit, low, cosine[j]))
        one.append(jnp.where(bit, cosine[j], up))
    at = [row_places.index(place) for place in range(7)]
    sub = iota((8, 128), 0)
    value = None
    for place in range(3):
        j = at[place]
        factor = jnp.where(((sub >> place) & 1) == 1, one[j], zero[j])
        value = factor if value is None else value * factor
    for place in range(3, 7):
        j = at[place]
        value = jnp.concatenate([value * zero[j], value * one[j]], axis=0)
    return value


def closing_rows(cosine, sine):
    lane = iota((128, 128), 1)
    row = iota((128, 128), 0)
    value = jnp.where((row >> 4) == (lane >> 4), 1.0, 0.0)
    for j in range(4):
        up = (row >> j) & 1
        across = (lane >> j) & 1
        value = value * jnp.where(up == across, cosine[j], jnp.where(up > across, sine[j], -sine[j]))
    return value


def row_gate(left, value):
    high, low = halves(value)
    out = jnp.dot(left, jnp.concatenate([high, low], axis=0), preferred_element_type=F32)
    return out[:128] + out[128:]


def lane_gate(right, value):
    high, low = halves(value)
    out = jnp.dot(jnp.concatenate([high, low], axis=1), right, preferred_element_type=F32)
    return out[:, :128] + out[:, 128:]


def store_row_matrix(ref, slot, matrix):
    high, low = halves(matrix)
    ref[slot] = jnp.concatenate(
        [jnp.concatenate([high, high], axis=1), jnp.concatenate([low, low], axis=1)], axis=0
    )


def store_lane_matrix(ref, slot, matrix):
    high, low = halves(matrix)
    both = jnp.concatenate([high, low], axis=1)
    ref[slot] = jnp.concatenate([both, both], axis=0)


def kernel(
    x_hbm, angles_hbm, masks_hbm, controls_hbm, final_hbm, out,
    x_v, angles, masks, controls, final,
    mid, send1, recv1, send2, recv2, signs, row_mats, lane_mats,
    in_sem, own_sem, send_sem, recv_sem,
):
    qa = lax.axis_index("qa")
    qb = lax.axis_index("qb")
    me = qa * 16 + qb
    loads = [
        pltpu.make_async_copy(source, place, in_sem.at[slot])
        for slot, (source, place) in enumerate((
            (angles_hbm, angles), (masks_hbm, masks), (controls_hbm, controls),
            (final_hbm, final), (x_hbm, x_v)))
    ]
    for load in loads:
        load.start()

    x, zh = lax.div(qa, 2), lax.rem(qa, 2)
    y, zl, core = lax.div(qb, 4), lax.rem(lax.div(qb, 2), 2), lax.rem(qb, 2)
    z = zh * 2 + zl
    way = 1 - 2 * core
    columns = [lax.rem(x + 4 + way * dx, 4) * 32 for dx in range(4)]
    lines = [lax.rem(y + 4 + way * dy, 4) * 4 for dy in range(4)]
    levels = [lax.rem(z + 4 + way * dz, 4) for dz in range(4)]
    cores = [core, 1 - core]
    inner = [[lax.div(tz, 2) * 16 + lax.rem(tz, 2) * 2 + tc for tc in cores] for tz in levels]
    outer = [[column + line for line in lines] for column in columns]

    def everyone(action, order):
        for dx, dy, dz, dc in order:
            action(outer[dx][dy] + inner[dz][dc])

    barrier = pltpu.get_barrier_semaphore()
    everyone(lambda target: pl.semaphore_signal(
        barrier, inc=1, device_id=target, device_id_type=pl.DeviceIdType.LOGICAL), FAR_FIRST)
    for load in loads[:4]:
        load.wait()

    lane1 = iota((1, 128), 1)
    mask_lanes = jnp.zeros((1, 128), jnp.int32)
    for layer in range(2):
        for gate in range(4):
            mask_lanes = jnp.where(lane1 == layer * 4 + gate, masks[layer, gate], mask_lanes)
    row = iota((128, 128), 0)
    sign_nat = 1.0 - 2.0 * gate_parity(row, NATURAL, mask_lanes).astype(F32)
    sign_mov = 1.0 - 2.0 * gate_parity(row, MOVED, mask_lanes).astype(F32)
    cos_all = [jnp.cos(angles[layer] * 0.5) for layer in range(2)]
    sin_all = [jnp.sin(angles[layer] * 0.5) for layer in range(2)]

    def splats(table, gate):
        return [jnp.broadcast_to(table[gate:gate + 1, j:j + 1], (1, 128)) for j in range(7)]

    def row_matrix(layer, gate, row_places, col_places):
        value = kron_rows(splats(cos_all[layer], gate), splats(sin_all[layer], gate), row_places, col_places, False)
        sign = sign_nat if row_places is NATURAL else sign_mov
        column = layer * 4 + gate
        return value * sign[:, column:column + 1]

    def lane_matrix(layer):
        value = kron_rows(splats(cos_all[layer], 0), splats(sin_all[layer], 0), NATURAL, NATURAL, True)
        return value * (1.0 - 2.0 * gate_parity(lane1, NATURAL, masks[layer, 0]).astype(F32))

    def parity_at(layer, position):
        parity = None
        for gate in range(4):
            term = (position >> STARTS[gate]) & (position >> controls[layer, gate])
            parity = term if parity is None else parity ^ term
        return parity & 1

    store_lane_matrix(lane_mats, 0, lane_matrix(0))
    store_row_matrix(row_mats, 0, row_matrix(0, 1, MOVED, NATURAL))
    store_row_matrix(row_mats, 1, row_matrix(0, 2, NATURAL, NATURAL))
    lanes8, sub8 = iota((8, 128), 1), iota((8, 128), 0)
    column = iota((128, 128), 1)
    parity = parity_at(0, row * 128 + column + me * 262144)
    first_signs = jnp.where(parity == 1, -1.0, 1.0)
    loads[4].wait()
    for pair in range(8):
        blocks = []
        for i in range(2):
            a = pair * 2 + i
            bits = [((a * 16384) >> controls[0, gate]) & 1 for gate in range(4)]
            flip = (bits[0] & lanes8) ^ (bits[1] & sub8) ^ (bits[3] & core)
            even = jnp.where((flip & 1) == 1, -1.0, 1.0)
            odd = jnp.where(((flip ^ bits[2]) & 1) == 1, -1.0, 1.0)
            factor = jnp.concatenate([even, even, odd, odd] * 4, axis=0)
            blocks.append(x_v[a * 128:(a + 1) * 128, :] * first_signs * factor)
        mixed = lane_gate(lane_mats[0], jnp.concatenate(blocks, axis=0))
        out_pair = row_gate(row_mats[0], jnp.concatenate([mixed[:128], mixed[128:]], axis=1))
        for i in range(2):
            a = pair * 2 + i
            mid[:, a * 8:(a + 1) * 8, :] = out_pair[:, i * 128:(i + 1) * 128].reshape(16, 8, 128)

    for k in range(0, 16, 2):
        mixed = row_gate(row_mats[1], jnp.concatenate([mid[k], mid[k + 1]], axis=1))
        for i in range(2):
            part = mixed[:, i * 128:(i + 1) * 128].reshape(16, 8, 128)
            for a in range(16):
                at = ((a // 2) * 16 + k + i) * 8
                send1[a % 2, at:at + 8, :] = part[a]
    pl.semaphore_wait(barrier, 127)

    def rows_of(device):
        return pl.ds(pl.multiple_of(device * 8, 8), 8)

    def ship(stage, chunk, source, landing):
        slot = stage * 2 + chunk
        own = pltpu.make_async_copy(
            source.at[chunk, rows_of(me)], landing.at[chunk, rows_of(me)], own_sem.at[slot])
        own.start()
        everyone(lambda target: pltpu.make_async_remote_copy(
            source.at[chunk, rows_of(target)], landing.at[chunk, rows_of(me)],
            send_sem.at[slot], recv_sem.at[slot],
            device_id=target, device_id_type=pl.DeviceIdType.LOGICAL).start(), SENDS)

    def landed(stage, chunk, source, landing):
        slot = stage * 2 + chunk
        pltpu.make_async_copy(
            source.at[chunk, rows_of(me)], landing.at[chunk, rows_of(me)], own_sem.at[slot]).wait()
        others = landing.at[chunk, pl.ds(0, 127 * 8)]
        pltpu.make_async_copy(others, others, recv_sem.at[slot]).wait()

    ship(0, 0, send1, recv1)
    ship(0, 1, send1, recv1)

    store_row_matrix(row_mats, 2, row_matrix(0, 3, NATURAL, NATURAL))
    store_lane_matrix(lane_mats, 1, lane_matrix(1))
    final_half = jnp.zeros((1, 128), F32)
    for j in range(4):
        final_half = jnp.where(lane1 == j, final[j] * 0.5, final_half)
    final_cos, final_sin = jnp.cos(final_half), jnp.sin(final_half)
    closing = closing_rows(
        [jnp.broadcast_to(final_cos[:, j:j + 1], (1, 128)) for j in range(4)],
        [jnp.broadcast_to(final_sin[:, j:j + 1], (1, 128)) for j in range(4)])
    store_row_matrix(row_mats, 6, closing)
    top = row_matrix(1, 3, NATURAL, NATURAL)
    store_row_matrix(row_mats, 3, row_gate(row_mats[6], jnp.concatenate([top, top], axis=1))[:, :128])
    store_row_matrix(row_mats, 4, row_matrix(1, 1, MOVED, MOVED))
    store_row_matrix(row_mats, 5, row_matrix(1, 2, NATURAL, NATURAL))
    here = lax.rem(me, 16) * 128 + lax.div(me, 16) * 32768
    device_spot = row * 262144 + iota((128, 128), 1) + here

    def layer_signs(block, carry):
        spots = device_spot + (lax.div(block, 8) * 16384 + lax.rem(block, 8) * 2048)
        signs[block] = jnp.where(parity_at(1, spots) == 1, -1.0, 1.0)
        return carry

    lax.fori_loop(0, 16, layer_signs, 0)

    for chunk in range(2):
        landed(0, chunk, send1, recv1)
        values = []
        for m in range(0, 8, 2):
            value = jnp.concatenate(
                [recv1[chunk, pl.ds(m + i, 128, stride=8), :] for i in range(2)], axis=1)
            values.append(row_gate(row_mats[2], value))
        for pair in range(4):
            value, block = values[pair], chunk * 8 + pair * 2
            value = jnp.concatenate(
                [value[:, :128] * signs[block], value[:, 128:] * signs[block + 1]], axis=0)
            value = lane_gate(lane_mats[1], value)
            values[pair] = jnp.concatenate([value[:128], value[128:]], axis=1)
        for pair in range(4):
            value = row_gate(row_mats[3], values[pair])
            for i in range(2):
                send2[chunk, pl.ds(pair * 2 + i, 128, stride=8), :] = value[:, i * 128:(i + 1) * 128]
        ship(1, chunk, send2, recv2)

    for chunk in range(2):
        landed(1, chunk, send2, recv2)
        for pair in range(4):
            at = pair * 256
            blocks = [recv2[chunk, at:at + 128, :], recv2[chunk, at + 128:at + 256, :]]
            out_pair = row_gate(row_mats[4], jnp.concatenate(blocks, axis=1))
            for i in range(2):
                a = (pair * 2 + i) * 2 + chunk
                mid[:, a * 8:(a + 1) * 8, :] = out_pair[:, i * 128:(i + 1) * 128].reshape(16, 8, 128)
    for k in range(0, 16, 2):
        mixed = row_gate(row_mats[5], jnp.concatenate([mid[k], mid[k + 1]], axis=1))
        for i in range(2):
            out[pl.ds(k + i, 128, stride=16), :] = mixed[:, i * 128:(i + 1) * 128]
    for slot in range(4):
        source = (send1, send2)[slot // 2]
        others = source.at[slot % 2, pl.ds(0, 127 * 8)]
        pltpu.make_async_copy(others, others, send_sem.at[slot]).wait()


def shards(amplitudes, gate_angles, pair_masks, control_qubits, final_angles):
    out = pl.pallas_call(
        kernel,
        out_shape=jax.ShapeDtypeStruct((2048, 128), F32),
        in_specs=[pl.BlockSpec(memory_space=pltpu.HBM)] * 5,
        out_specs=pl.BlockSpec(memory_space=pltpu.VMEM),
        scratch_shapes=[
            pltpu.VMEM((2048, 128), F32),
            pltpu.VMEM(gate_angles.shape, F32),
            pltpu.SMEM(pair_masks.shape, jnp.int32),
            pltpu.SMEM(control_qubits.shape, jnp.int32),
            pltpu.SMEM(final_angles.shape, F32),
            pltpu.VMEM((16, 128, 128), F32),
            pltpu.VMEM((2, 1024, 128), F32),
            pltpu.VMEM((2, 1024, 128), F32),
            pltpu.VMEM((2, 1024, 128), F32),
            pltpu.VMEM((2, 1024, 128), F32),
            pltpu.VMEM((16, 128, 128), F32),
            pltpu.VMEM((7, 256, 256), BF16),
            pltpu.VMEM((2, 256, 256), BF16),
            pltpu.SemaphoreType.DMA((5,)),
            pltpu.SemaphoreType.DMA((4,)),
            pltpu.SemaphoreType.DMA((4,)),
            pltpu.SemaphoreType.DMA((4,)),
        ],
        compiler_params=pltpu.CompilerParams(
            collective_id=0, has_side_effects=True, vmem_limit_bytes=24 * 2**20),
        name="layers",
    )(*(pltpu.with_memory_space_constraint(value, pltpu.HBM) for value in (
        amplitudes.reshape(2048, 128), gate_angles, pair_masks, control_qubits, final_angles)))
    return out.reshape(amplitudes.shape)


def solution(mesh):
    return jax.shard_map(
        shards,
        mesh=mesh,
        in_specs=(P("qa", "qb", None), P(), P(), P(), P()),
        out_specs=P("qa", "qb", None),
        check_vma=False,
    )
```

```python
import jax
import jax.numpy as jnp
from jax import lax
from jax.sharding import PartitionSpec as P
from jax.experimental import pallas as pl
from jax.experimental.pallas import tpu as pltpu

F32 = jnp.float32
BF16 = jnp.bfloat16
NATURAL = (0, 1, 2, 3, 4, 5, 6)
MOVED = (3, 4, 5, 6, 0, 1, 2)
STARTS = (0, 7, 11, 18)
FIXED = (-1, -2)
STEPS = [(n // 32, n // 8 % 4, n // 2 % 4, n % 2) for n in range(1, 128)]


def hops(step):
    return sum(min(part, 4 - part) for part in step[:3])


def spread(step):
    return (step[0] * 32 + step[1] * 8 + step[2] * 2 + step[3]) * 53 % 128


def first_axis(step):
    return 0 if step[0] else 1 if step[1] else 2


def merged(steps):
    placed = []
    for kind in range(3):
        group = [step for step in steps if first_axis(step) == kind]
        placed += [((n + 0.5) / len(group), step) for n, step in enumerate(group)]
    return [step for _, step in sorted(placed)]


FAR_FIRST = sorted(STEPS, key=lambda step: (-hops(step), spread(step)))
SENDS = merged(FAR_FIRST)


def iota(shape, dim):
    return lax.broadcasted_iota(jnp.int32, shape, dim)


def halves(value):
    high = value.astype(BF16)
    return high, (value - high.astype(F32)).astype(BF16)


def gate_parity(index, places, mask):
    bits = [index >> places[j] for j in range(7)]
    parity = None
    pair = 0
    for j in range(6):
        inner = None
        for k in range(j + 1, 7):
            term = (mask >> pair) & bits[k]
            inner = term if inner is None else inner ^ term
            pair += 1
        term = inner & bits[j]
        parity = term if parity is None else parity ^ term
    return parity & 1


def kron_rows(cosine, sine, row_places, col_places, flip):
    lane = iota((1, 128), 1)
    zero, one = [], []
    for j in range(7):
        low, up = (sine[j], -sine[j]) if flip else (-sine[j], sine[j])
        if col_places[j] < 0:
            fixed = col_places[j] == FIXED[1]
            zero.append(low if fixed else cosine[j])
            one.append(cosine[j] if fixed else up)
            continue
        bit = ((lane >> col_places[j]) & 1) == 1
        zero.append(jnp.where(bit, low, cosine[j]))
        one.append(jnp.where(bit, cosine[j], up))
    at = [row_places.index(place) for place in range(7)]
    sub = iota((8, 128), 0)
    value = None
    for place in range(3):
        j = at[place]
        factor = jnp.where(((sub >> place) & 1) == 1, one[j], zero[j])
        value = factor if value is None else value * factor
    for place in range(3, 7):
        j = at[place]
        value = jnp.concatenate([value * zero[j], value * one[j]], axis=0)
    return value


def closing_rows(cosine, sine):
    lane = iota((128, 128), 1)
    row = iota((128, 128), 0)
    value = jnp.where((row >> 4) == (lane >> 4), 1.0, 0.0)
    for j in range(4):
        up = (row >> j) & 1
        across = (lane >> j) & 1
        value = value * jnp.where(up == across, cosine[j], jnp.where(up > across, sine[j], -sine[j]))
    return value


def row_gate(left, value):
    high, low = halves(value)
    out = jnp.dot(left, jnp.concatenate([high, low], axis=0), preferred_element_type=F32)
    return out[:128] + out[128:]


def lane_gate(right, value):
    high, low = halves(value)
    out = jnp.dot(jnp.concatenate([high, low], axis=1), right, preferred_element_type=F32)
    return out[:, :128] + out[:, 128:]


def store_row_matrix(ref, slot, matrix):
    high, low = halves(matrix)
    ref[slot] = jnp.concatenate(
        [jnp.concatenate([high, high], axis=1), jnp.concatenate([low, low], axis=1)], axis=0
    )


def store_lane_matrix(ref, slot, matrix):
    high, low = halves(matrix)
    both = jnp.concatenate([high, low], axis=1)
    ref[slot] = jnp.concatenate([both, both], axis=0)


def kernel(
    x_hbm, angles_hbm, masks_hbm, controls_hbm, final_hbm, out,
    x_v, angles, masks, controls, final,
    mid, send1, recv1, send2, recv2, signs, row_mats, lane_mats, split_mats,
    in_sem, own_sem, send_sem, recv_sem,
):
    qa = lax.axis_index("qa")
    qb = lax.axis_index("qb")
    me = qa * 16 + qb
    loads = [
        pltpu.make_async_copy(source, place, in_sem.at[slot])
        for slot, (source, place) in enumerate((
            (angles_hbm, angles), (masks_hbm, masks), (controls_hbm, controls),
            (final_hbm, final), (x_hbm, x_v)))
    ]
    for load in loads:
        load.start()

    x, zh = lax.div(qa, 2), lax.rem(qa, 2)
    y, zl, core = lax.div(qb, 4), lax.rem(lax.div(qb, 2), 2), lax.rem(qb, 2)
    z = zh * 2 + zl
    way = 1 - 2 * core
    columns = [lax.rem(x + 4 + way * dx, 4) * 32 for dx in range(4)]
    lines = [lax.rem(y + 4 + way * dy, 4) * 4 for dy in range(4)]
    levels = [lax.rem(z + 4 + way * dz, 4) for dz in range(4)]
    cores = [core, 1 - core]
    inner = [[lax.div(tz, 2) * 16 + lax.rem(tz, 2) * 2 + tc for tc in cores] for tz in levels]
    outer = [[column + line for line in lines] for column in columns]

    def everyone(action, order):
        for dx, dy, dz, dc in order:
            action(outer[dx][dy] + inner[dz][dc])

    barrier = pltpu.get_barrier_semaphore()
    everyone(lambda target: pl.semaphore_signal(
        barrier, inc=1, device_id=target, device_id_type=pl.DeviceIdType.LOGICAL), FAR_FIRST)
    for load in loads[:4]:
        load.wait()

    lane1 = iota((1, 128), 1)
    mask_lanes = jnp.zeros((1, 128), jnp.int32)
    for layer in range(2):
        for gate in range(4):
            mask_lanes = jnp.where(lane1 == layer * 4 + gate, masks[layer, gate], mask_lanes)
    row = iota((128, 128), 0)
    sign_nat = 1.0 - 2.0 * gate_parity(row, NATURAL, mask_lanes).astype(F32)
    sign_mov = 1.0 - 2.0 * gate_parity(row, MOVED, mask_lanes).astype(F32)
    cos_all = [jnp.cos(angles[layer] * 0.5) for layer in range(2)]
    sin_all = [jnp.sin(angles[layer] * 0.5) for layer in range(2)]

    def splats(table, gate):
        return [jnp.broadcast_to(table[gate:gate + 1, j:j + 1], (1, 128)) for j in range(7)]

    def row_matrix(layer, gate, row_places, col_places):
        value = kron_rows(splats(cos_all[layer], gate), splats(sin_all[layer], gate), row_places, col_places, False)
        sign = sign_nat if row_places is NATURAL else sign_mov
        column = layer * 4 + gate
        return value * sign[:, column:column + 1]

    def lane_matrix(layer):
        value = kron_rows(splats(cos_all[layer], 0), splats(sin_all[layer], 0), NATURAL, NATURAL, True)
        return value * (1.0 - 2.0 * gate_parity(lane1, NATURAL, masks[layer, 0]).astype(F32))

    def parity_at(layer, position):
        parity = None
        for gate in range(4):
            term = (position >> STARTS[gate]) & (position >> controls[layer, gate])
            parity = term if parity is None else parity ^ term
        return parity & 1

    store_lane_matrix(lane_mats, 0, lane_matrix(0))
    store_row_matrix(row_mats, 0, row_matrix(0, 1, MOVED, NATURAL))
    store_row_matrix(row_mats, 1, row_matrix(0, 2, NATURAL, NATURAL))
    lanes8, sub8 = iota((8, 128), 1), iota((8, 128), 0)
    column = iota((128, 128), 1)
    parity = parity_at(0, row * 128 + column + me * 262144)
    first_signs = jnp.where(parity == 1, -1.0, 1.0)
    loads[4].wait()
    for pair in range(8):
        blocks = []
        for i in range(2):
            a = pair * 2 + i
            bits = [((a * 16384) >> controls[0, gate]) & 1 for gate in range(4)]
            flip = (bits[0] & lanes8) ^ (bits[1] & sub8) ^ (bits[3] & core)
            even = jnp.where((flip & 1) == 1, -1.0, 1.0)
            odd = jnp.where(((flip ^ bits[2]) & 1) == 1, -1.0, 1.0)
            factor = jnp.concatenate([even, even, odd, odd] * 4, axis=0)
            blocks.append(x_v[a * 128:(a + 1) * 128, :] * first_signs * factor)
        mixed = lane_gate(lane_mats[0], jnp.concatenate(blocks, axis=0))
        out_pair = row_gate(row_mats[0], jnp.concatenate([mixed[:128], mixed[128:]], axis=1))
        for i in range(2):
            a = pair * 2 + i
            mid[:, a * 8:(a + 1) * 8, :] = out_pair[:, i * 128:(i + 1) * 128].reshape(16, 8, 128)

    for k in range(0, 16, 2):
        mixed = row_gate(row_mats[1], jnp.concatenate([mid[k], mid[k + 1]], axis=1))
        for i in range(2):
            part = mixed[:, i * 128:(i + 1) * 128].reshape(16, 8, 128)
            for a in range(16):
                at = ((a // 2) * 16 + k + i) * 8
                send1[a % 2, at:at + 8, :] = part[a]
    pl.semaphore_wait(barrier, 127)

    def rows_of(device):
        return pl.ds(pl.multiple_of(device * 8, 8), 8)

    def ship(stage, chunk, source, landing):
        slot = stage * 2 + chunk
        own = pltpu.make_async_copy(
            source.at[chunk, rows_of(me)], landing.at[chunk, rows_of(me)], own_sem.at[slot])
        own.start()
        everyone(lambda target: pltpu.make_async_remote_copy(
            source.at[chunk, rows_of(target)], landing.at[chunk, rows_of(me)],
            send_sem.at[slot], recv_sem.at[slot],
            device_id=target, device_id_type=pl.DeviceIdType.LOGICAL).start(), SENDS)

    def landed(stage, chunk, source, landing):
        slot = stage * 2 + chunk
        pltpu.make_async_copy(
            source.at[chunk, rows_of(me)], landing.at[chunk, rows_of(me)], own_sem.at[slot]).wait()
        others = landing.at[chunk, pl.ds(0, 127 * 8)]
        pltpu.make_async_copy(others, others, recv_sem.at[slot]).wait()

    ship(0, 0, send1, recv1)
    ship(0, 1, send1, recv1)

    store_row_matrix(row_mats, 2, row_matrix(0, 3, NATURAL, NATURAL))
    store_lane_matrix(lane_mats, 1, lane_matrix(1))
    final_half = jnp.zeros((1, 128), F32)
    for j in range(4):
        final_half = jnp.where(lane1 == j, final[j] * 0.5, final_half)
    final_cos, final_sin = jnp.cos(final_half), jnp.sin(final_half)
    closing = closing_rows(
        [jnp.broadcast_to(final_cos[:, j:j + 1], (1, 128)) for j in range(4)],
        [jnp.broadcast_to(final_sin[:, j:j + 1], (1, 128)) for j in range(4)])
    store_row_matrix(row_mats, 6, closing)
    top = row_matrix(1, 3, NATURAL, NATURAL)
    store_row_matrix(row_mats, 3, row_gate(row_mats[6], jnp.concatenate([top, top], axis=1))[:, :128])
    store_row_matrix(row_mats, 4, row_matrix(1, 1, MOVED, MOVED))
    for chunk in range(2):
        high, low = halves(row_matrix(1, 2, NATURAL, (0, 1, 2, FIXED[chunk], 3, 4, 5)))
        split_mats[chunk] = jnp.concatenate([high, low], axis=1)
    here = lax.rem(me, 16) * 128 + lax.div(me, 16) * 32768
    device_spot = row * 262144 + iota((128, 128), 1) + here

    def layer_signs(block, carry):
        spots = device_spot + (lax.div(block, 8) * 16384 + lax.rem(block, 8) * 2048)
        signs[block] = jnp.where(parity_at(1, spots) == 1, -1.0, 1.0)
        return carry

    lax.fori_loop(0, 16, layer_signs, 0)

    for chunk in range(2):
        landed(0, chunk, send1, recv1)
        values = []
        for m in range(0, 8, 2):
            value = jnp.concatenate(
                [recv1[chunk, pl.ds(m + i, 128, stride=8), :] for i in range(2)], axis=1)
            values.append(row_gate(row_mats[2], value))
        for pair in range(4):
            value, block = values[pair], chunk * 8 + pair * 2
            value = jnp.concatenate(
                [value[:, :128] * signs[block], value[:, 128:] * signs[block + 1]], axis=0)
            value = lane_gate(lane_mats[1], value)
            values[pair] = jnp.concatenate([value[:128], value[128:]], axis=1)
        for pair in range(4):
            value = row_gate(row_mats[3], values[pair])
            for i in range(2):
                send2[chunk, pl.ds(pair * 2 + i, 128, stride=8), :] = value[:, i * 128:(i + 1) * 128]
        ship(1, chunk, send2, recv2)

    for chunk in range(2):
        landed(1, chunk, send2, recv2)
        for pair in range(4):
            at = pair * 256
            blocks = [recv2[chunk, at:at + 128, :], recv2[chunk, at + 128:at + 256, :]]
            out_pair = row_gate(row_mats[4], jnp.concatenate(blocks, axis=1))
            for i in range(2):
                at = chunk * 64 + (pair * 2 + i) * 8
                mid[:, at:at + 8, :] = out_pair[:, i * 128:(i + 1) * 128].reshape(16, 8, 128)
        for k in range(0, 16, 2):
            rows = slice(chunk * 64, chunk * 64 + 64)
            high, low = halves(jnp.concatenate([mid[k, rows], mid[k + 1, rows]], axis=1))
            mixed = jnp.dot(
                split_mats[chunk], jnp.concatenate([high, low, high, low], axis=0), preferred_element_type=F32)
            for i in range(2):
                part = mixed[:, i * 128:(i + 1) * 128]
                if chunk == 0:
                    signs[k + i] = part
                else:
                    out[pl.ds(k + i, 128, stride=16), :] = signs[k + i] + part
    for slot in range(4):
        source = (send1, send2)[slot // 2]
        others = source.at[slot % 2, pl.ds(0, 127 * 8)]
        pltpu.make_async_copy(others, others, send_sem.at[slot]).wait()


def shards(amplitudes, gate_angles, pair_masks, control_qubits, final_angles):
    out = pl.pallas_call(
        kernel,
        out_shape=jax.ShapeDtypeStruct((2048, 128), F32),
        in_specs=[pl.BlockSpec(memory_space=pltpu.HBM)] * 5,
        out_specs=pl.BlockSpec(memory_space=pltpu.VMEM),
        scratch_shapes=[
            pltpu.VMEM((2048, 128), F32),
            pltpu.VMEM(gate_angles.shape, F32),
            pltpu.SMEM(pair_masks.shape, jnp.int32),
            pltpu.SMEM(control_qubits.shape, jnp.int32),
            pltpu.SMEM(final_angles.shape, F32),
            pltpu.VMEM((16, 128, 128), F32),
            pltpu.VMEM((2, 1024, 128), F32),
            pltpu.VMEM((2, 1024, 128), F32),
            pltpu.VMEM((2, 1024, 128), F32),
            pltpu.VMEM((2, 1024, 128), F32),
            pltpu.VMEM((16, 128, 128), F32),
            pltpu.VMEM((7, 256, 256), BF16),
            pltpu.VMEM((2, 256, 256), BF16),
            pltpu.VMEM((2, 128, 256), BF16),
            pltpu.SemaphoreType.DMA((5,)),
            pltpu.SemaphoreType.DMA((4,)),
            pltpu.SemaphoreType.DMA((4,)),
            pltpu.SemaphoreType.DMA((4,)),
        ],
        compiler_params=pltpu.CompilerParams(
            collective_id=0, has_side_effects=True, vmem_limit_bytes=24 * 2**20),
        name="layers",
    )(*(pltpu.with_memory_space_constraint(value, pltpu.HBM) for value in (
        amplitudes.reshape(2048, 128), gate_angles, pair_masks, control_qubits, final_angles)))
    return out.reshape(amplitudes.shape)


def solution(mesh):
    return jax.shard_map(
        shards,
        mesh=mesh,
        in_specs=(P("qa", "qb", None), P(), P(), P(), P()),
        out_specs=P("qa", "qb", None),
        check_vma=False,
    )
```

```python
import jax
import jax.numpy as jnp
from jax import lax
from jax.sharding import PartitionSpec as P
from jax.experimental import pallas as pl
from jax.experimental.pallas import tpu as pltpu

F32 = jnp.float32
BF16 = jnp.bfloat16
NATURAL = (0, 1, 2, 3, 4, 5, 6)
MOVED = (3, 4, 5, 6, 0, 1, 2)
STARTS = (0, 7, 11, 18)
FIXED = (-1, -2)
STEPS = [(n // 32, n // 8 % 4, n // 2 % 4, n % 2) for n in range(1, 128)]


def hops(step):
    return sum(min(part, 4 - part) for part in step[:3])


def spread(step):
    return (step[0] * 32 + step[1] * 8 + step[2] * 2 + step[3]) * 53 % 128


def first_axis(step):
    return 0 if step[0] else 1 if step[1] else 2


def merged(steps):
    placed = []
    for kind in range(3):
        group = [step for step in steps if first_axis(step) == kind]
        placed += [((n + 0.5) / len(group), step) for n, step in enumerate(group)]
    return [step for _, step in sorted(placed)]


FAR_FIRST = sorted(STEPS, key=lambda step: (-hops(step), spread(step)))
SENDS = merged(FAR_FIRST)


def iota(shape, dim):
    return lax.broadcasted_iota(jnp.int32, shape, dim)


def halves(value):
    high = value.astype(BF16)
    return high, (value - high.astype(F32)).astype(BF16)


def gate_parity(index, places, mask):
    bits = [index >> places[j] for j in range(7)]
    parity = None
    pair = 0
    for j in range(6):
        inner = None
        for k in range(j + 1, 7):
            term = (mask >> pair) & bits[k]
            inner = term if inner is None else inner ^ term
            pair += 1
        term = inner & bits[j]
        parity = term if parity is None else parity ^ term
    return parity & 1


def kron_rows(cosine, sine, row_places, col_places, flip):
    lane = iota((1, 128), 1)
    zero, one = [], []
    for j in range(7):
        low, up = (sine[j], -sine[j]) if flip else (-sine[j], sine[j])
        if col_places[j] < 0:
            fixed = col_places[j] == FIXED[1]
            zero.append(low if fixed else cosine[j])
            one.append(cosine[j] if fixed else up)
            continue
        bit = ((lane >> col_places[j]) & 1) == 1
        zero.append(jnp.where(bit, low, cosine[j]))
        one.append(jnp.where(bit, cosine[j], up))
    at = [row_places.index(place) for place in range(7)]
    sub = iota((8, 128), 0)
    value = None
    for place in range(3):
        j = at[place]
        factor = jnp.where(((sub >> place) & 1) == 1, one[j], zero[j])
        value = factor if value is None else value * factor
    for place in range(3, 7):
        j = at[place]
        value = jnp.concatenate([value * zero[j], value * one[j]], axis=0)
    return value


def closing_rows(cosine, sine):
    lane = iota((128, 128), 1)
    row = iota((128, 128), 0)
    value = jnp.where((row >> 4) == (lane >> 4), 1.0, 0.0)
    for j in range(4):
        up = (row >> j) & 1
        across = (lane >> j) & 1
        value = value * jnp.where(up == across, cosine[j], jnp.where(up > across, sine[j], -sine[j]))
    return value


def row_gate(left, value):
    high, low = halves(value)
    out = jnp.dot(left, jnp.concatenate([high, low], axis=0), preferred_element_type=F32)
    return out[:128] + out[128:]


def lane_gate(right, value):
    high, low = halves(value)
    out = jnp.dot(jnp.concatenate([high, low], axis=1), right, preferred_element_type=F32)
    return out[:, :128] + out[:, 128:]


def half_gate(left, first, second):
    high, low = halves(jnp.concatenate([first, second], axis=1))
    return jnp.dot(left, jnp.concatenate([high, low, high, low], axis=0), preferred_element_type=F32)


def store_row_matrix(ref, slot, matrix):
    high, low = halves(matrix)
    ref[slot] = jnp.concatenate(
        [jnp.concatenate([high, high], axis=1), jnp.concatenate([low, low], axis=1)], axis=0
    )


def store_lane_matrix(ref, slot, matrix):
    high, low = halves(matrix)
    both = jnp.concatenate([high, low], axis=1)
    ref[slot] = jnp.concatenate([both, both], axis=0)


def kernel(
    x_hbm, angles_hbm, masks_hbm, controls_hbm, final_hbm, mid, signs, split_mats,
    x_v, angles, masks, controls, final,
    send1, recv1, send2, recv2, row_mats, lane_mats,
    in_sem, own_sem, send_sem, recv_sem,
):
    qa = lax.axis_index("qa")
    qb = lax.axis_index("qb")
    me = qa * 16 + qb
    loads = [
        pltpu.make_async_copy(source, place, in_sem.at[slot])
        for slot, (source, place) in enumerate((
            (angles_hbm, angles), (masks_hbm, masks), (controls_hbm, controls),
            (final_hbm, final), (x_hbm, x_v)))
    ]
    for load in loads:
        load.start()

    x, zh = lax.div(qa, 2), lax.rem(qa, 2)
    y, zl, core = lax.div(qb, 4), lax.rem(lax.div(qb, 2), 2), lax.rem(qb, 2)
    z = zh * 2 + zl
    way = 1 - 2 * core
    columns = [lax.rem(x + 4 + way * dx, 4) * 32 for dx in range(4)]
    lines = [lax.rem(y + 4 + way * dy, 4) * 4 for dy in range(4)]
    levels = [lax.rem(z + 4 + way * dz, 4) for dz in range(4)]
    cores = [core, 1 - core]
    inner = [[lax.div(tz, 2) * 16 + lax.rem(tz, 2) * 2 + tc for tc in cores] for tz in levels]
    outer = [[column + line for line in lines] for column in columns]

    def everyone(action, order):
        for dx, dy, dz, dc in order:
            action(outer[dx][dy] + inner[dz][dc])

    barrier = pltpu.get_barrier_semaphore()
    everyone(lambda target: pl.semaphore_signal(
        barrier, inc=1, device_id=target, device_id_type=pl.DeviceIdType.LOGICAL), FAR_FIRST)
    for load in loads[:4]:
        load.wait()

    lane1 = iota((1, 128), 1)
    mask_lanes = jnp.zeros((1, 128), jnp.int32)
    for layer in range(2):
        for gate in range(4):
            mask_lanes = jnp.where(lane1 == layer * 4 + gate, masks[layer, gate], mask_lanes)
    row = iota((128, 128), 0)
    sign_nat = 1.0 - 2.0 * gate_parity(row, NATURAL, mask_lanes).astype(F32)
    sign_mov = 1.0 - 2.0 * gate_parity(row, MOVED, mask_lanes).astype(F32)
    cos_all = [jnp.cos(angles[layer] * 0.5) for layer in range(2)]
    sin_all = [jnp.sin(angles[layer] * 0.5) for layer in range(2)]

    def splats(table, gate):
        return [jnp.broadcast_to(table[gate:gate + 1, j:j + 1], (1, 128)) for j in range(7)]

    def row_matrix(layer, gate, row_places, col_places):
        value = kron_rows(splats(cos_all[layer], gate), splats(sin_all[layer], gate), row_places, col_places, False)
        sign = sign_nat if row_places is NATURAL else sign_mov
        column = layer * 4 + gate
        return value * sign[:, column:column + 1]

    def lane_matrix(layer):
        value = kron_rows(splats(cos_all[layer], 0), splats(sin_all[layer], 0), NATURAL, NATURAL, True)
        return value * (1.0 - 2.0 * gate_parity(lane1, NATURAL, masks[layer, 0]).astype(F32))

    def parity_at(layer, position):
        parity = None
        for gate in range(4):
            term = (position >> STARTS[gate]) & (position >> controls[layer, gate])
            parity = term if parity is None else parity ^ term
        return parity & 1

    store_lane_matrix(lane_mats, 0, lane_matrix(0))
    store_row_matrix(row_mats, 0, row_matrix(0, 1, MOVED, NATURAL))
    store_row_matrix(row_mats, 1, row_matrix(0, 2, NATURAL, NATURAL))
    lanes8, sub8 = iota((8, 128), 1), iota((8, 128), 0)
    column = iota((128, 128), 1)
    parity = parity_at(0, row * 128 + column + me * 262144)
    first_signs = jnp.where(parity == 1, -1.0, 1.0)
    loads[4].wait()
    for pair in range(8):
        blocks = []
        for i in range(2):
            a = pair * 2 + i
            bits = [((a * 16384) >> controls[0, gate]) & 1 for gate in range(4)]
            flip = (bits[0] & lanes8) ^ (bits[1] & sub8) ^ (bits[3] & core)
            even = jnp.where((flip & 1) == 1, -1.0, 1.0)
            odd = jnp.where(((flip ^ bits[2]) & 1) == 1, -1.0, 1.0)
            factor = jnp.concatenate([even, even, odd, odd] * 4, axis=0)
            blocks.append(x_v[a * 128:(a + 1) * 128, :] * first_signs * factor)
        mixed = lane_gate(lane_mats[0], jnp.concatenate(blocks, axis=0))
        out_pair = row_gate(row_mats[0], jnp.concatenate([mixed[:128], mixed[128:]], axis=1))
        for i in range(2):
            a = pair * 2 + i
            mid[:, a * 8:(a + 1) * 8, :] = out_pair[:, i * 128:(i + 1) * 128].reshape(16, 8, 128)

    for k in range(0, 16, 2):
        mixed = row_gate(row_mats[1], jnp.concatenate([mid[k], mid[k + 1]], axis=1))
        for i in range(2):
            part = mixed[:, i * 128:(i + 1) * 128].reshape(16, 8, 128)
            for a in range(16):
                at = ((a // 2) * 16 + k + i) * 8
                send1[a % 2, at:at + 8, :] = part[a]
    pl.semaphore_wait(barrier, 127)

    def rows_of(device):
        return pl.ds(pl.multiple_of(device * 8, 8), 8)

    def ship(stage, chunk, source, landing):
        slot = stage * 2 + chunk
        own = pltpu.make_async_copy(
            source.at[chunk, rows_of(me)], landing.at[chunk, rows_of(me)], own_sem.at[slot])
        own.start()
        everyone(lambda target: pltpu.make_async_remote_copy(
            source.at[chunk, rows_of(target)], landing.at[chunk, rows_of(me)],
            send_sem.at[slot], recv_sem.at[slot],
            device_id=target, device_id_type=pl.DeviceIdType.LOGICAL).start(), SENDS)

    def landed(stage, chunk, source, landing):
        slot = stage * 2 + chunk
        pltpu.make_async_copy(
            source.at[chunk, rows_of(me)], landing.at[chunk, rows_of(me)], own_sem.at[slot]).wait()
        others = landing.at[chunk, pl.ds(0, 127 * 8)]
        pltpu.make_async_copy(others, others, recv_sem.at[slot]).wait()

    ship(0, 0, send1, recv1)
    ship(0, 1, send1, recv1)

    store_row_matrix(row_mats, 2, row_matrix(0, 3, NATURAL, NATURAL))
    store_lane_matrix(lane_mats, 1, lane_matrix(1))
    final_half = jnp.zeros((1, 128), F32)
    for j in range(4):
        final_half = jnp.where(lane1 == j, final[j] * 0.5, final_half)
    final_cos, final_sin = jnp.cos(final_half), jnp.sin(final_half)
    closing = closing_rows(
        [jnp.broadcast_to(final_cos[:, j:j + 1], (1, 128)) for j in range(4)],
        [jnp.broadcast_to(final_sin[:, j:j + 1], (1, 128)) for j in range(4)])
    store_row_matrix(row_mats, 6, closing)
    top = row_matrix(1, 3, NATURAL, NATURAL)
    store_row_matrix(row_mats, 3, row_gate(row_mats[6], jnp.concatenate([top, top], axis=1))[:, :128])
    store_row_matrix(row_mats, 4, row_matrix(1, 1, MOVED, MOVED))
    for chunk in range(2):
        high, low = halves(row_matrix(1, 2, NATURAL, (0, 1, 2, FIXED[chunk], 3, 4, 5)))
        split_mats[chunk] = jnp.concatenate([high, low], axis=1)
    here = lax.rem(me, 16) * 128 + lax.div(me, 16) * 32768
    device_spot = row * 262144 + iota((128, 128), 1) + here

    def layer_signs(block, carry):
        spots = device_spot + (lax.div(block, 8) * 16384 + lax.rem(block, 8) * 2048)
        signs[block] = jnp.where(parity_at(1, spots) == 1, -1.0, 1.0)
        return carry

    lax.fori_loop(0, 16, layer_signs, 0)

    for chunk in range(2):
        landed(0, chunk, send1, recv1)
        values = []
        for m in range(0, 8, 2):
            value = jnp.concatenate(
                [recv1[chunk, pl.ds(m + i, 128, stride=8), :] for i in range(2)], axis=1)
            values.append(row_gate(row_mats[2], value))
        for pair in range(4):
            value, block = values[pair], chunk * 8 + pair * 2
            value = jnp.concatenate(
                [value[:, :128] * signs[block], value[:, 128:] * signs[block + 1]], axis=0)
            value = lane_gate(lane_mats[1], value)
            values[pair] = jnp.concatenate([value[:128], value[128:]], axis=1)
        for pair in range(4):
            value = row_gate(row_mats[3], values[pair])
            for i in range(2):
                send2[chunk, pl.ds(pair * 2 + i, 128, stride=8), :] = value[:, i * 128:(i + 1) * 128]
        ship(1, chunk, send2, recv2)

    for chunk in range(2):
        landed(1, chunk, send2, recv2)
        for pair in range(4):
            at = pair * 256
            blocks = [recv2[chunk, at:at + 128, :], recv2[chunk, at + 128:at + 256, :]]
            out_pair = row_gate(row_mats[4], jnp.concatenate(blocks, axis=1))
            for i in range(2):
                at = chunk * 64 + (pair * 2 + i) * 8
                mid[:, at:at + 8, :] = out_pair[:, i * 128:(i + 1) * 128].reshape(16, 8, 128)
        if chunk == 0:
            for k in range(0, 16, 2):
                mixed = half_gate(split_mats[0], mid[k, 0:64], mid[k + 1, 0:64])
                for i in range(2):
                    signs[k + i] = mixed[:, i * 128:(i + 1) * 128]
    for slot in range(4):
        source = (send1, send2)[slot // 2]
        others = source.at[slot % 2, pl.ds(0, 127 * 8)]
        pltpu.make_async_copy(others, others, send_sem.at[slot]).wait()


def finish(mid, sums, split_mats, out_hbm, rows, out_sem):
    shaped = rows.reshape(128, 16, 128)
    copies = []
    for k in range(0, 16, 2):
        mixed = half_gate(split_mats[1], mid[k, 64:128], mid[k + 1, 64:128])
        for i in range(2):
            rows[pl.ds(k + i, 128, stride=16), :] = sums[k + i] + mixed[:, i * 128:(i + 1) * 128]
        if k % 8 == 6:
            part = slice(k - 6, k + 2)
            copies.append(pltpu.make_async_copy(shaped.at[:, part], out_hbm.at[:, part], out_sem.at[k // 8]))
            copies[-1].start()
    for copy in copies:
        copy.wait()


def shards(amplitudes, gate_angles, pair_masks, control_qubits, final_angles):
    parts = pl.pallas_call(
        kernel,
        out_shape=(
            jax.ShapeDtypeStruct((16, 128, 128), F32),
            jax.ShapeDtypeStruct((16, 128, 128), F32),
            jax.ShapeDtypeStruct((2, 128, 256), BF16),
        ),
        in_specs=[pl.BlockSpec(memory_space=pltpu.HBM)] * 5,
        out_specs=[pl.BlockSpec(memory_space=pltpu.VMEM)] * 3,
        scratch_shapes=[
            pltpu.VMEM((2048, 128), F32),
            pltpu.VMEM(gate_angles.shape, F32),
            pltpu.SMEM(pair_masks.shape, jnp.int32),
            pltpu.SMEM(control_qubits.shape, jnp.int32),
            pltpu.SMEM(final_angles.shape, F32),
            pltpu.VMEM((2, 1024, 128), F32),
            pltpu.VMEM((2, 1024, 128), F32),
            pltpu.VMEM((2, 1024, 128), F32),
            pltpu.VMEM((2, 1024, 128), F32),
            pltpu.VMEM((7, 256, 256), BF16),
            pltpu.VMEM((2, 256, 256), BF16),
            pltpu.SemaphoreType.DMA((5,)),
            pltpu.SemaphoreType.DMA((4,)),
            pltpu.SemaphoreType.DMA((4,)),
            pltpu.SemaphoreType.DMA((4,)),
        ],
        compiler_params=pltpu.CompilerParams(
            collective_id=0, has_side_effects=True, vmem_limit_bytes=24 * 2**20),
        name="layers",
    )(*(pltpu.with_memory_space_constraint(value, pltpu.HBM) for value in (
        amplitudes.reshape(2048, 128), gate_angles, pair_masks, control_qubits, final_angles)))
    out = pl.pallas_call(
        finish,
        out_shape=jax.ShapeDtypeStruct((128, 16, 128), F32),
        in_specs=[pl.BlockSpec(memory_space=pltpu.VMEM)] * 3,
        out_specs=pl.BlockSpec(memory_space=pl.ANY),
        scratch_shapes=[pltpu.VMEM((2048, 128), F32), pltpu.SemaphoreType.DMA((2,))],
        compiler_params=pltpu.CompilerParams(vmem_limit_bytes=8 * 2**20),
        name="finish",
    )(*parts)
    return out.reshape(amplitudes.shape)


def solution(mesh):
    return jax.shard_map(
        shards,
        mesh=mesh,
        in_specs=(P("qa", "qb", None), P(), P(), P(), P()),
        out_specs=P("qa", "qb", None),
        check_vma=False,
    )
```

```python
import jax
import jax.numpy as jnp
from jax import lax
from jax.sharding import PartitionSpec as P
from jax.experimental import pallas as pl
from jax.experimental.pallas import tpu as pltpu

F32 = jnp.float32
BF16 = jnp.bfloat16
NATURAL = (0, 1, 2, 3, 4, 5, 6)
MOVED = (3, 4, 5, 6, 0, 1, 2)
STARTS = (0, 7, 11, 18)
FIXED = (-1, -2)
STEPS = [(n // 32, n // 8 % 4, n // 2 % 4, n % 2) for n in range(1, 128)]


def hops(step):
    return sum(min(part, 4 - part) for part in step[:3])


def spread(step):
    return (step[0] * 32 + step[1] * 8 + step[2] * 2 + step[3]) * 53 % 128


def first_axis(step):
    return 0 if step[0] else 1 if step[1] else 2


def merged(steps):
    placed = []
    for kind in range(3):
        group = [step for step in steps if first_axis(step) == kind]
        placed += [((n + 0.5) / len(group) * (0.8, 0.9, 1)[kind], step) for n, step in enumerate(group)]
    return [step for _, step in sorted(placed)]


FAR_FIRST = sorted(STEPS, key=lambda step: (-hops(step), spread(step)))
SENDS = merged(FAR_FIRST)


def iota(shape, dim):
    return lax.broadcasted_iota(jnp.int32, shape, dim)


def halves(value):
    high = value.astype(BF16)
    return high, (value - high.astype(F32)).astype(BF16)


def gate_parity(index, places, mask):
    bits = [index >> places[j] for j in range(7)]
    parity = None
    pair = 0
    for j in range(6):
        inner = None
        for k in range(j + 1, 7):
            term = (mask >> pair) & bits[k]
            inner = term if inner is None else inner ^ term
            pair += 1
        term = inner & bits[j]
        parity = term if parity is None else parity ^ term
    return parity & 1


def kron_rows(cosine, sine, row_places, col_places, flip):
    lane = iota((1, 128), 1)
    zero, one = [], []
    for j in range(7):
        low, up = (sine[j], -sine[j]) if flip else (-sine[j], sine[j])
        if col_places[j] < 0:
            fixed = col_places[j] == FIXED[1]
            zero.append(low if fixed else cosine[j])
            one.append(cosine[j] if fixed else up)
            continue
        bit = ((lane >> col_places[j]) & 1) == 1
        zero.append(jnp.where(bit, low, cosine[j]))
        one.append(jnp.where(bit, cosine[j], up))
    at = [row_places.index(place) for place in range(7)]
    sub = iota((8, 128), 0)
    value = None
    for place in range(3):
        j = at[place]
        factor = jnp.where(((sub >> place) & 1) == 1, one[j], zero[j])
        value = factor if value is None else value * factor
    for place in range(3, 7):
        j = at[place]
        value = jnp.concatenate([value * zero[j], value * one[j]], axis=0)
    return value


def closing_rows(cosine, sine):
    lane = iota((128, 128), 1)
    row = iota((128, 128), 0)
    value = jnp.where((row >> 4) == (lane >> 4), 1.0, 0.0)
    for j in range(4):
        up = (row >> j) & 1
        across = (lane >> j) & 1
        value = value * jnp.where(up == across, cosine[j], jnp.where(up > across, sine[j], -sine[j]))
    return value


def row_gate(left, value):
    high, low = halves(value)
    out = jnp.dot(left, jnp.concatenate([high, low], axis=0), preferred_element_type=F32)
    return out[:128] + out[128:]


def lane_gate(right, value):
    high, low = halves(value)
    out = jnp.dot(jnp.concatenate([high, low], axis=1), right, preferred_element_type=F32)
    return out[:, :128] + out[:, 128:]


def half_gate(left, first, second):
    high, low = halves(jnp.concatenate([first, second], axis=1))
    return jnp.dot(left, jnp.concatenate([high, low, high, low], axis=0), preferred_element_type=F32)


def store_row_matrix(ref, slot, matrix):
    high, low = halves(matrix)
    ref[slot] = jnp.concatenate(
        [jnp.concatenate([high, high], axis=1), jnp.concatenate([low, low], axis=1)], axis=0
    )


def store_lane_matrix(ref, slot, matrix):
    high, low = halves(matrix)
    both = jnp.concatenate([high, low], axis=1)
    ref[slot] = jnp.concatenate([both, both], axis=0)


def kernel(
    x_hbm, angles_hbm, masks_hbm, controls_hbm, final_hbm, mid, signs, split_mats,
    x_v, angles, masks, controls, final,
    send1, recv1, send2, recv2, row_mats, lane_mats,
    in_sem, own_sem, send_sem, recv_sem,
):
    qa = lax.axis_index("qa")
    qb = lax.axis_index("qb")
    me = qa * 16 + qb
    loads = [
        pltpu.make_async_copy(source, place, in_sem.at[slot])
        for slot, (source, place) in enumerate((
            (angles_hbm, angles), (masks_hbm, masks), (controls_hbm, controls),
            (final_hbm, final), (x_hbm, x_v)))
    ]
    for load in loads:
        load.start()

    x, zh = lax.div(qa, 2), lax.rem(qa, 2)
    y, zl, core = lax.div(qb, 4), lax.rem(lax.div(qb, 2), 2), lax.rem(qb, 2)
    z = zh * 2 + zl
    way = 1 - 2 * core
    columns = [lax.rem(x + 4 + way * dx, 4) * 32 for dx in range(4)]
    lines = [lax.rem(y + 4 + way * dy, 4) * 4 for dy in range(4)]
    levels = [lax.rem(z + 4 + way * dz, 4) for dz in range(4)]
    cores = [core, 1 - core]
    inner = [[lax.div(tz, 2) * 16 + lax.rem(tz, 2) * 2 + tc for tc in cores] for tz in levels]
    outer = [[column + line for line in lines] for column in columns]

    def everyone(action, order):
        for dx, dy, dz, dc in order:
            action(outer[dx][dy] + inner[dz][dc])

    barrier = pltpu.get_barrier_semaphore()
    everyone(lambda target: pl.semaphore_signal(
        barrier, inc=1, device_id=target, device_id_type=pl.DeviceIdType.LOGICAL), FAR_FIRST)
    for load in loads[:4]:
        load.wait()

    lane1 = iota((1, 128), 1)
    mask_lanes = jnp.zeros((1, 128), jnp.int32)
    for layer in range(2):
        for gate in range(4):
            mask_lanes = jnp.where(lane1 == layer * 4 + gate, masks[layer, gate], mask_lanes)
    row = iota((128, 128), 0)
    sign_nat = 1.0 - 2.0 * gate_parity(row, NATURAL, mask_lanes).astype(F32)
    sign_mov = 1.0 - 2.0 * gate_parity(row, MOVED, mask_lanes).astype(F32)
    cos_all = [jnp.cos(angles[layer] * 0.5) for layer in range(2)]
    sin_all = [jnp.sin(angles[layer] * 0.5) for layer in range(2)]

    def splats(table, gate):
        return [jnp.broadcast_to(table[gate:gate + 1, j:j + 1], (1, 128)) for j in range(7)]

    def row_matrix(layer, gate, row_places, col_places):
        value = kron_rows(splats(cos_all[layer], gate), splats(sin_all[layer], gate), row_places, col_places, False)
        sign = sign_nat if row_places is NATURAL else sign_mov
        column = layer * 4 + gate
        return value * sign[:, column:column + 1]

    def lane_matrix(layer):
        value = kron_rows(splats(cos_all[layer], 0), splats(sin_all[layer], 0), NATURAL, NATURAL, True)
        return value * (1.0 - 2.0 * gate_parity(lane1, NATURAL, masks[layer, 0]).astype(F32))

    def parity_at(layer, position):
        parity = None
        for gate in range(4):
            term = (position >> STARTS[gate]) & (position >> controls[layer, gate])
            parity = term if parity is None else parity ^ term
        return parity & 1

    store_lane_matrix(lane_mats, 0, lane_matrix(0))
    store_row_matrix(row_mats, 0, row_matrix(0, 1, MOVED, NATURAL))
    store_row_matrix(row_mats, 1, row_matrix(0, 2, NATURAL, NATURAL))
    lanes8, sub8 = iota((8, 128), 1), iota((8, 128), 0)
    column = iota((128, 128), 1)
    parity = parity_at(0, row * 128 + column + me * 262144)
    first_signs = jnp.where(parity == 1, -1.0, 1.0)
    loads[4].wait()
    for pair in range(8):
        blocks = []
        for i in range(2):
            a = pair * 2 + i
            bits = [((a * 16384) >> controls[0, gate]) & 1 for gate in range(4)]
            flip = (bits[0] & lanes8) ^ (bits[1] & sub8) ^ (bits[3] & core)
            even = jnp.where((flip & 1) == 1, -1.0, 1.0)
            odd = jnp.where(((flip ^ bits[2]) & 1) == 1, -1.0, 1.0)
            factor = jnp.concatenate([even, even, odd, odd] * 4, axis=0)
            blocks.append(x_v[a * 128:(a + 1) * 128, :] * first_signs * factor)
        mixed = lane_gate(lane_mats[0], jnp.concatenate(blocks, axis=0))
        out_pair = row_gate(row_mats[0], jnp.concatenate([mixed[:128], mixed[128:]], axis=1))
        for i in range(2):
            a = pair * 2 + i
            mid[:, a * 8:(a + 1) * 8, :] = out_pair[:, i * 128:(i + 1) * 128].reshape(16, 8, 128)

    for k in range(0, 16, 2):
        mixed = row_gate(row_mats[1], jnp.concatenate([mid[k], mid[k + 1]], axis=1))
        for i in range(2):
            part = mixed[:, i * 128:(i + 1) * 128].reshape(16, 8, 128)
            for a in range(16):
                at = ((a // 2) * 16 + k + i) * 8
                send1[a % 2, at:at + 8, :] = part[a]
    pl.semaphore_wait(barrier, 127)

    def rows_of(device):
        return pl.ds(pl.multiple_of(device * 8, 8), 8)

    def ship(stage, chunk, source, landing):
        slot = stage * 2 + chunk
        own = pltpu.make_async_copy(
            source.at[chunk, rows_of(me)], landing.at[chunk, rows_of(me)], own_sem.at[slot])
        own.start()
        everyone(lambda target: pltpu.make_async_remote_copy(
            source.at[chunk, rows_of(target)], landing.at[chunk, rows_of(me)],
            send_sem.at[slot], recv_sem.at[slot],
            device_id=target, device_id_type=pl.DeviceIdType.LOGICAL).start(), SENDS)

    def landed(stage, chunk, source, landing):
        slot = stage * 2 + chunk
        pltpu.make_async_copy(
            source.at[chunk, rows_of(me)], landing.at[chunk, rows_of(me)], own_sem.at[slot]).wait()
        others = landing.at[chunk, pl.ds(0, 127 * 8)]
        pltpu.make_async_copy(others, others, recv_sem.at[slot]).wait()

    ship(0, 0, send1, recv1)
    ship(0, 1, send1, recv1)

    store_row_matrix(row_mats, 2, row_matrix(0, 3, NATURAL, NATURAL))
    store_lane_matrix(lane_mats, 1, lane_matrix(1))
    final_half = jnp.zeros((1, 128), F32)
    for j in range(4):
        final_half = jnp.where(lane1 == j, final[j] * 0.5, final_half)
    final_cos, final_sin = jnp.cos(final_half), jnp.sin(final_half)
    closing = closing_rows(
        [jnp.broadcast_to(final_cos[:, j:j + 1], (1, 128)) for j in range(4)],
        [jnp.broadcast_to(final_sin[:, j:j + 1], (1, 128)) for j in range(4)])
    store_row_matrix(row_mats, 6, closing)
    top = row_matrix(1, 3, NATURAL, NATURAL)
    store_row_matrix(row_mats, 3, row_gate(row_mats[6], jnp.concatenate([top, top], axis=1))[:, :128])
    store_row_matrix(row_mats, 4, row_matrix(1, 1, MOVED, MOVED))
    for chunk in range(2):
        high, low = halves(row_matrix(1, 2, NATURAL, (0, 1, 2, FIXED[chunk], 3, 4, 5)))
        split_mats[chunk] = jnp.concatenate([high, low], axis=1)
    here = lax.rem(me, 16) * 128 + lax.div(me, 16) * 32768
    device_spot = row * 262144 + iota((128, 128), 1) + here

    def layer_signs(block, carry):
        spots = device_spot + (lax.div(block, 8) * 16384 + lax.rem(block, 8) * 2048)
        signs[block] = jnp.where(parity_at(1, spots) == 1, -1.0, 1.0)
        return carry

    lax.fori_loop(0, 16, layer_signs, 0)

    for chunk in range(2):
        landed(0, chunk, send1, recv1)
        values = []
        for m in range(0, 8, 2):
            value = jnp.concatenate(
                [recv1[chunk, pl.ds(m + i, 128, stride=8), :] for i in range(2)], axis=1)
            values.append(row_gate(row_mats[2], value))
        for pair in range(4):
            value, block = values[pair], chunk * 8 + pair * 2
            value = jnp.concatenate(
                [value[:, :128] * signs[block], value[:, 128:] * signs[block + 1]], axis=0)
            value = lane_gate(lane_mats[1], value)
            values[pair] = jnp.concatenate([value[:128], value[128:]], axis=1)
        for pair in range(4):
            value = row_gate(row_mats[3], values[pair])
            for i in range(2):
                send2[chunk, pl.ds(pair * 2 + i, 128, stride=8), :] = value[:, i * 128:(i + 1) * 128]
        ship(1, chunk, send2, recv2)

    for chunk in range(2):
        for slot in (0, 1, 2) if chunk == 0 else (3,):
            others = (send1, send2)[slot // 2].at[slot % 2, pl.ds(0, 127 * 8)]
            pltpu.make_async_copy(others, others, send_sem.at[slot]).wait()
        landed(1, chunk, send2, recv2)
        for pair in range(4):
            at = pair * 256
            blocks = [recv2[chunk, at:at + 128, :], recv2[chunk, at + 128:at + 256, :]]
            out_pair = row_gate(row_mats[4], jnp.concatenate(blocks, axis=1))
            for i in range(2):
                at = chunk * 64 + (pair * 2 + i) * 8
                mid[:, at:at + 8, :] = out_pair[:, i * 128:(i + 1) * 128].reshape(16, 8, 128)
        if chunk == 0:
            for k in range(0, 16, 2):
                mixed = half_gate(split_mats[0], mid[k, 0:64], mid[k + 1, 0:64])
                for i in range(2):
                    signs[k + i] = mixed[:, i * 128:(i + 1) * 128]


def finish(mid, sums, split_mats, out_hbm, rows, out_sem):
    shaped = rows.reshape(128, 16, 128)
    copies = []
    for k in range(0, 16, 2):
        mixed = half_gate(split_mats[1], mid[k, 64:128], mid[k + 1, 64:128])
        for i in range(2):
            rows[pl.ds(k + i, 128, stride=16), :] = sums[k + i] + mixed[:, i * 128:(i + 1) * 128]
        if k % 8 == 6:
            part = slice(k - 6, k + 2)
            copies.append(pltpu.make_async_copy(shaped.at[:, part], out_hbm.at[:, part], out_sem.at[k // 8]))
            copies[-1].start()
    for copy in copies:
        copy.wait()


def shards(amplitudes, gate_angles, pair_masks, control_qubits, final_angles):
    parts = pl.pallas_call(
        kernel,
        out_shape=(
            jax.ShapeDtypeStruct((16, 128, 128), F32),
            jax.ShapeDtypeStruct((16, 128, 128), F32),
            jax.ShapeDtypeStruct((2, 128, 256), BF16),
        ),
        in_specs=[pl.BlockSpec(memory_space=pltpu.HBM)] * 5,
        out_specs=[pl.BlockSpec(memory_space=pltpu.VMEM)] * 3,
        scratch_shapes=[
            pltpu.VMEM((2048, 128), F32),
            pltpu.VMEM(gate_angles.shape, F32),
            pltpu.SMEM(pair_masks.shape, jnp.int32),
            pltpu.SMEM(control_qubits.shape, jnp.int32),
            pltpu.SMEM(final_angles.shape, F32),
            pltpu.VMEM((2, 1024, 128), F32),
            pltpu.VMEM((2, 1024, 128), F32),
            pltpu.VMEM((2, 1024, 128), F32),
            pltpu.VMEM((2, 1024, 128), F32),
            pltpu.VMEM((7, 256, 256), BF16),
            pltpu.VMEM((2, 256, 256), BF16),
            pltpu.SemaphoreType.DMA((5,)),
            pltpu.SemaphoreType.DMA((4,)),
            pltpu.SemaphoreType.DMA((4,)),
            pltpu.SemaphoreType.DMA((4,)),
        ],
        compiler_params=pltpu.CompilerParams(
            collective_id=0, has_side_effects=True, vmem_limit_bytes=24 * 2**20),
        name="layers",
    )(*(pltpu.with_memory_space_constraint(value, pltpu.HBM) for value in (
        amplitudes.reshape(2048, 128), gate_angles, pair_masks, control_qubits, final_angles)))
    out = pl.pallas_call(
        finish,
        out_shape=jax.ShapeDtypeStruct((128, 16, 128), F32),
        in_specs=[pl.BlockSpec(memory_space=pltpu.VMEM)] * 3,
        out_specs=pl.BlockSpec(memory_space=pl.ANY),
        scratch_shapes=[pltpu.VMEM((2048, 128), F32), pltpu.SemaphoreType.DMA((2,))],
        compiler_params=pltpu.CompilerParams(vmem_limit_bytes=8 * 2**20),
        name="finish",
    )(*parts)
    return out.reshape(amplitudes.shape)


def solution(mesh):
    return jax.shard_map(
        shards,
        mesh=mesh,
        in_specs=(P("qa", "qb", None), P(), P(), P(), P()),
        out_specs=P("qa", "qb", None),
        check_vma=False,
    )
```
